256 devices in a mesh: tok: 64 (over z, x, core), fsdp: 4 (over y).
Axes of the slice: x: 4, y: 4, z: 8, core: 2. Of those that a mesh axis runs over, the one named last changes fastest.
Arguments:
- tokens: bfloat16 [49152, 2048], P('tok'), may hold values from -6 to 6
- attn_gain: float32 [2048], replicated, may hold values from 0.1 to 1.9
- w_query: bfloat16 [2048, 16, 64], P('tok', 'fsdp'), as said below
- key_value_weight: bfloat16 [2048, 2, 4, 64], P('tok', None, 'fsdp'), may hold values from -0.125 to 0.125
- w_out: bfloat16 [16, 64, 2048], P('fsdp', None, 'tok'), may hold values from -0.1875 to 0.1875
- mlp_gain: float32 [2048], replicated, may hold values from 0.1 to 1.9
- w_gate: bfloat16 [2048, 4096], P('tok', 'fsdp'), may hold values from -0.125 to 0.125
- w_up: bfloat16 [2048, 4096], P('tok', 'fsdp'), may hold values from -0.125 to 0.125
- w_down: bfloat16 [4096, 2048], P('fsdp', 'tok'), may hold values from -0.09375 to 0.09375
- doc_lengths: int32 [256], replicated, may hold values from 1 to 768, 49152 in all
Outputs:
- layer_out: bfloat16 [49152, 2048], P('tok')
The draws below stay inside these ranges and needn't reach their ends.
Inputs may be any that keep to these rules, and one draw needn't show every extreme that they name: `doc_lengths`: the documents fill the batch in order and their lengths sum to 49152. `w_query`: entries are centred at zero.
All inputs are finite; a program needn't handle non-finite values.
Results may differ from the reference program's by a relative error of at most 0.02.
The reference program's roundings to bfloat16 on the way count: a program that leaves them out, or rounds other values in their place, can miss the bound.
Values may be sent and summed in bfloat16 or wider, within the bound.
A program may use at most 64 MiB of HBM per device.

```python
import math
import jax
import jax.numpy as jnp
import numpy as np
from jax import lax

MODEL_WIDTH = 2048
QUERY_HEADS = 16
KEY_VALUE_HEADS = 4
HEAD_WIDTH = 64
FF = 4096
TOKENS_PER_SHARD = 768
PACKED_TOKENS = 49152
NDOC = 256
N_TOK = 64
N_FSDP = 4


def draw_w_query(key, part):
    key = jax.random.fold_in(key, 7)
    entries = jnp.clip(jax.random.normal(key, (MODEL_WIDTH, QUERY_HEADS, HEAD_WIDTH), jnp.float32), -6.0, 6.0) * MODEL_WIDTH ** (-0.5)
    return entries.astype(jnp.bfloat16)


def steps_of(key, dims, cuts, low, largest):
    factor_of, own = 1.0, jax.random.fold_in(key, 6)
    for dim, shards_of in cuts:
        draws = jnp.exp(jax.random.uniform(jax.random.fold_in(own, dim), (shards_of,), jnp.float32, low / len(cuts), largest / len(cuts)))
        factor_of = factor_of * jnp.repeat(draws, dims[dim] // shards_of).reshape([-1 if axis == dim else 1 for axis in range(len(dims))])
    return factor_of


def split_up(count, total, reach, skew):
    portions = [(1 << 20) // math.isqrt(grade ** skew) + 1 for grade in range(2, count + 1)]
    surplus, counts = total - reach - (count - 1), [1] * (count - 1)
    while surplus > 0:
        candidates = [i for i in range(count - 1) if counts[i] < reach]
        whole, remaining = sum([portions[i] for i in candidates]), surplus
        for i in candidates:
            extra = min(reach - counts[i], max(1, remaining * portions[i] // whole), surplus)
            counts[i] = counts[i] + extra
            surplus = surplus - extra
    return np.array([reach] + counts)


def uneven(key, number_of, total, bound, lean):
    if number_of == 2:
        one = jax.random.randint(key, (), max(1, total - bound), min(bound, total - 1) + 1)
        return jnp.stack([one, total - one])
    sizes = jnp.asarray(split_up(number_of, total, bound, lean), jnp.int32)
    pairs = (number_of - 1) // 2
    giver, taker = sizes[1:1 + 2 * pairs:2], sizes[2:2 + 2 * pairs:2]
    slack = jnp.minimum(giver - 1, bound - taker)
    moved = jax.random.randint(jax.random.fold_in(key, 1), (pairs,), 0, 1 << 20) % (slack + 1)
    sizes = sizes.at[1:1 + 2 * pairs:2].set(giver - moved).at[2:2 + 2 * pairs:2].set(taker + moved)
    return sizes[jax.random.permutation(jax.random.fold_in(key, 2), number_of)]


def centred(own_key, shape, deviation, reach, pieces=(), kind=jnp.bfloat16):
    result = jax.random.normal(own_key, shape, jnp.float32) * deviation
    if len(pieces) > 0:
        result = steps_of(own_key, shape, pieces, -0.22, 0.18) * result
    return jnp.clip(result, min=-reach, max=reach).astype(kind)


def setup_inputs(seed: int = 0) -> dict:
    streams_of = jax.random.split(jax.random.key(seed), 11)
    return {
        "tokens": centred(streams_of[0], (PACKED_TOKENS, MODEL_WIDTH), 1.0, 6.0, ((0, 64),)),
        "attn_gain": jnp.clip(1.0 + 0.18 * jax.random.normal(streams_of[1], (MODEL_WIDTH,), jnp.float32), 0.1, 1.9),
        "w_query": draw_w_query(jax.random.fold_in(streams_of[10], 71), 0),
        "key_value_weight": centred(streams_of[3], (MODEL_WIDTH, 2, KEY_VALUE_HEADS, HEAD_WIDTH), MODEL_WIDTH ** -0.5, 0.125, ((0, 64), (2, 4))),
        "w_out": centred(streams_of[4], (QUERY_HEADS, HEAD_WIDTH, MODEL_WIDTH), (QUERY_HEADS * HEAD_WIDTH) ** -0.5, 0.1875, ((0, 4), (2, 64))),
        "mlp_gain": jnp.clip(1.0 + 0.18 * jax.random.normal(streams_of[5], (MODEL_WIDTH,), jnp.float32), 0.1, 1.9),
        "w_gate": centred(streams_of[6], (MODEL_WIDTH, FF), MODEL_WIDTH ** -0.5, 0.125, ((0, 64), (1, 4))),
        "w_up": centred(streams_of[7], (MODEL_WIDTH, FF), MODEL_WIDTH ** -0.5, 0.125, ((0, 64), (1, 4))),
        "w_down": centred(streams_of[8], (FF, MODEL_WIDTH), FF ** -0.5, 0.09375, ((0, 4), (1, 64))),
        "doc_lengths": uneven(streams_of[9], NDOC, PACKED_TOKENS, TOKENS_PER_SHARD, 2).astype(jnp.int32),
    }


ROPE_BASE = 500000.0
NORM_EPS = 1e-05
MASKED = -1e+30

def rms_norm(values, gain):
    wide = values.astype(jnp.float32)
    factor = lax.rsqrt(lax.optimization_barrier(jnp.mean(wide * wide, axis=-1, keepdims=True)) + NORM_EPS)
    return (wide * factor * gain.astype(jnp.float32)).astype(jnp.bfloat16)

def doc_starts(positions, doc_lengths):
    doc_ends = jnp.cumsum(doc_lengths)
    passed = doc_ends[None, :] <= positions[:, None]
    return lax.optimization_barrier(jnp.sum(jnp.where(passed, doc_lengths[None, :], 0), axis=1)).astype(jnp.int32)

def rotate(values, offsets):
    half_size = values.shape[-1] // 2
    frequency = ROPE_BASE ** (-2.0 * jnp.arange(half_size, dtype=jnp.float32) / values.shape[-1])
    angles = offsets.astype(jnp.float32)[:, None] * frequency[None, :]
    cosine = jnp.cos(angles)[:, None, :]
    sine_part = jnp.sin(angles)[:, None, :]
    lead_part = values[..., :half_size]
    tail_part = values[..., half_size:]
    return jnp.concatenate([lead_part * cosine - tail_part * sine_part, tail_part * cosine + lead_part * sine_part], axis=-1)

def attend_ref(query_matrix, query_pos, query_start, key_part, value_part, key_pos):
    scores = jnp.einsum('qngd,knd->ngqk', query_matrix.astype(jnp.float32), key_part.astype(jnp.float32)) * HEAD_WIDTH ** (-0.5)
    allowed = (key_pos[None, :] >= query_start[:, None]) & (key_pos[None, :] <= query_pos[:, None])
    scores = jnp.where(allowed[None, None], scores, MASKED)
    row_max = lax.optimization_barrier(jnp.max(scores, axis=-1, keepdims=True))
    weights = jnp.exp(scores - row_max)
    totals = lax.optimization_barrier(jnp.sum(weights, axis=-1))
    rounded = weights.astype(jnp.bfloat16)
    blended = jnp.einsum('ngqk,knd->qngd', rounded.astype(jnp.float32), value_part.astype(jnp.float32))
    blended = blended / jnp.transpose(totals, (2, 0, 1))[..., None]
    return blended.reshape(query_matrix.shape[0], -1).astype(jnp.bfloat16)

def rounded_sum(partials):
    summed = jnp.zeros(partials[0].shape, jnp.float32)
    for partial_value in partials:
        narrow = lax.optimization_barrier(partial_value.astype(jnp.bfloat16))
        summed = summed + narrow.astype(jnp.float32)
    return summed

def reference(tokens, attn_gain, w_query, key_value_weight, w_out, mlp_gain, w_gate, w_up, w_down, doc_lengths):
    positions = jnp.arange(PACKED_TOKENS, dtype=jnp.int32)
    starts = doc_starts(positions, doc_lengths)
    offsets = positions - starts
    normed_input = rms_norm(tokens, attn_gain)
    query_matrix = jnp.dot(normed_input, w_query.reshape(MODEL_WIDTH, QUERY_HEADS * HEAD_WIDTH), preferred_element_type=jnp.float32).reshape(PACKED_TOKENS, QUERY_HEADS, HEAD_WIDTH)
    query_matrix = rotate(query_matrix, offsets).astype(jnp.bfloat16)
    paired_output = jnp.dot(normed_input, key_value_weight.reshape(MODEL_WIDTH, 2 * KEY_VALUE_HEADS * HEAD_WIDTH), preferred_element_type=jnp.float32).reshape(PACKED_TOKENS, 2, KEY_VALUE_HEADS, HEAD_WIDTH)
    rotated_keys = rotate(paired_output[:, 0], offsets).astype(jnp.bfloat16)
    value_matrix_rows = paired_output[:, 1].astype(jnp.bfloat16)
    query_group_width = QUERY_HEADS // KEY_VALUE_HEADS
    padded_keys = jnp.concatenate([jnp.zeros((TOKENS_PER_SHARD, KEY_VALUE_HEADS, HEAD_WIDTH), jnp.bfloat16), rotated_keys], axis=0)
    padded_values = jnp.concatenate([jnp.zeros((TOKENS_PER_SHARD, KEY_VALUE_HEADS, HEAD_WIDTH), jnp.bfloat16), value_matrix_rows], axis=0)

    def one_home(home_index):
        shifted_rows = (home_index * TOKENS_PER_SHARD).astype(jnp.int32)
        resident_query_rows = lax.dynamic_slice_in_dim(query_matrix, shifted_rows, TOKENS_PER_SHARD, 0).reshape(TOKENS_PER_SHARD, KEY_VALUE_HEADS, query_group_width, HEAD_WIDTH)
        query_pos = shifted_rows + jnp.arange(TOKENS_PER_SHARD, dtype=jnp.int32)
        query_start = lax.dynamic_slice_in_dim(starts, shifted_rows, TOKENS_PER_SHARD, 0)
        key_part = lax.dynamic_slice_in_dim(padded_keys, shifted_rows, 2 * TOKENS_PER_SHARD, 0)
        value_part = lax.dynamic_slice_in_dim(padded_values, shifted_rows, 2 * TOKENS_PER_SHARD, 0)
        key_pos = shifted_rows - TOKENS_PER_SHARD + jnp.arange(2 * TOKENS_PER_SHARD, dtype=jnp.int32)
        return attend_ref(resident_query_rows, query_pos, query_start, key_part, value_part, key_pos)
    attended = lax.map(one_home, jnp.arange(N_TOK, dtype=jnp.int32)).reshape(PACKED_TOKENS, QUERY_HEADS * HEAD_WIDTH)
    head_cols = QUERY_HEADS * HEAD_WIDTH // N_FSDP
    out_split = w_out.reshape(N_FSDP, head_cols, MODEL_WIDTH)
    attn_parts = []
    for member in range(N_FSDP):
        attn_parts.append(jnp.dot(attended[:, member * head_cols:(member + 1) * head_cols], out_split[member], preferred_element_type=jnp.float32))
    residual = (tokens.astype(jnp.float32) + rounded_sum(attn_parts)).astype(jnp.bfloat16)
    mlp_in = rms_norm(residual, mlp_gain)
    unit_cols = FF // N_FSDP
    mlp_parts = []
    for member in range(N_FSDP):
        gate_out = jnp.dot(mlp_in, w_gate[:, member * unit_cols:(member + 1) * unit_cols], preferred_element_type=jnp.float32)
        up_out = jnp.dot(mlp_in, w_up[:, member * unit_cols:(member + 1) * unit_cols], preferred_element_type=jnp.float32)
        hidden = (jax.nn.silu(gate_out) * up_out).astype(jnp.bfloat16)
        mlp_parts.append(jnp.dot(hidden, w_down[member * unit_cols:(member + 1) * unit_cols], preferred_element_type=jnp.float32))
    return (residual.astype(jnp.float32) + rounded_sum(mlp_parts)).astype(jnp.bfloat16)
```

```python
import functools

import jax
import jax.numpy as jnp
from jax import lax
from jax.experimental import pallas as pl
from jax.experimental.pallas import tpu as pltpu
from jax.sharding import PartitionSpec as P

ROPE_BASE = 500000.0
NORM_EPS = 1e-05
MASKED = -1e30
MESH = pl.DeviceIdType.MESH
F32, BF16 = jnp.float32, jnp.bfloat16

NZ, NX, NY = 8, 4, 4
ROWS = 768
WIDTH = 2048
HALF = 384
BLOCK = 96
SPAN = 512
UNITS = 4
WINDOW = 896
SEMS = 256


def nt(a, b):
    return lax.dot_general(a, b, (((1,), (1,)), ((), ())), preferred_element_type=F32)


def nn(a, b):
    return jnp.dot(a, b, preferred_element_type=F32)


class Net:
    def __init__(self, send_sem, recv_sem):
        tok, self.y = lax.axis_index("tok"), lax.axis_index("fsdp")
        self.c = lax.rem(tok, 2)
        self.x = lax.rem(tok // 2, NX)
        self.z = tok // (2 * NX)
        self.send_sem, self.recv_sem = send_sem, recv_sem
        self.copies = []
        z, x, c, y = self.z, self.x, self.c, self.y

        def at(z, x, c):
            return (z * NX + x) * 2 + c

        self.zp = (at(self.zs(1), x, c), y)
        self.zm = (at(self.zs(-1), x, c), y)
        self.xp = (at(z, self.xs(1), c), y)
        self.xm = (at(z, self.xs(-1), c), y)
        self.sib = (at(z, x, 1 - c), y)
        self.yp = (tok, self.ys(1))
        self.ym = (tok, self.ys(-1))
        self.y2 = (tok, self.ys(2))
        count = 2 * NX * NZ
        self.after = (lax.rem(tok + 1, count), y)
        self.before = (lax.rem(tok + count - 1, count), y)

    def zs(self, d):
        return lax.rem(self.z + NZ + d, NZ)

    def xs(self, d):
        return lax.rem(self.x + NX + d, NX)

    def ys(self, d):
        return lax.rem(self.y + NY + d, NY)

    def barrier(self):
        partners = [
            self.zp, self.zm, self.xp, self.xm, self.sib,
            self.yp, self.ym, self.y2, self.after, self.before,
        ]
        sem = pltpu.get_barrier_semaphore()
        for p in partners:
            pl.semaphore_signal(sem, 1, device_id=p, device_id_type=MESH)
        pl.semaphore_wait(sem, len(partners))

    def send(self, src, dst, to):
        i = len(self.copies)
        copy = pltpu.make_async_remote_copy(
            src_ref=src, dst_ref=dst, send_sem=self.send_sem.at[i],
            recv_sem=self.recv_sem.at[i], device_id=to, device_id_type=MESH,
        )
        copy.start()
        self.copies.append(copy)
        return copy

    def same(self, ref, to):
        return self.send(ref, ref, to)


def arrived(*copies):
    for copy in copies:
        copy.wait_recv()


def gather_xz(net, w):
    x, z, c, xs, zs = net.x, net.z, net.c, net.xs, net.zs
    sib = []
    a, b = net.same(w.at[z, x, c], net.xp), net.same(w.at[z, x, c], net.xm)
    yield
    arrived(a, b)
    a = net.same(w.at[z, xs(-1), c, pl.ds(0, 16)], net.xp)
    b = net.same(w.at[z, xs(1), c, pl.ds(16, 16)], net.xm)
    yield
    arrived(a, b)
    a, b = net.same(w.at[z, :, c], net.zp), net.same(w.at[z, :, c], net.zm)
    sib.append(net.same(w.at[z, :, c], net.sib))
    yield
    for hop in (1, 2):
        arrived(a, b)
        lo, hi = w.at[zs(-hop), :, c], w.at[zs(hop), :, c]
        a, b = net.same(lo, net.zp), net.same(hi, net.zm)
        sib += [net.same(lo, net.sib), net.same(hi, net.sib)]
        yield
    arrived(a, b)
    a = net.same(w.at[zs(-3), pl.ds(0, 2), c], net.zp)
    b = net.same(w.at[zs(3), pl.ds(2, 2), c], net.zm)
    sib += [net.same(w.at[zs(-3), :, c], net.sib), net.same(w.at[zs(3), :, c], net.sib)]
    yield
    arrived(a, b)
    sib.append(net.same(w.at[zs(4), :, c], net.sib))
    yield
    arrived(*sib)
    yield


def gather_zx(net, w):
    x, z, c, xs, zs = net.x, net.z, net.c, net.xs, net.zs
    a, b = net.same(w.at[z, x, c], net.zp), net.same(w.at[z, x, c], net.zm)
    yield
    for hop in (1, 2):
        arrived(a, b)
        a, b = net.same(w.at[zs(-hop), x, c], net.zp), net.same(w.at[zs(hop), x, c], net.zm)
        yield
    arrived(a, b)
    a = net.same(w.at[zs(-3), x, c, pl.ds(0, 16)], net.zp)
    b = net.same(w.at[zs(3), x, c, pl.ds(16, 16)], net.zm)
    yield
    arrived(a, b)
    a, b = net.same(w.at[:, x, c], net.xp), net.same(w.at[:, x, c], net.xm)
    sib = [net.same(w.at[:, x, c], net.sib)]
    yield
    arrived(a, b)
    lo, hi = xs(-1), xs(1)
    a = net.same(w.at[pl.ds(0, 4), lo, c], net.xp)
    b = net.same(w.at[pl.ds(4, 4), hi, c], net.xm)
    sib += [net.same(w.at[:, lo, c], net.sib), net.same(w.at[:, hi, c], net.sib)]
    yield
    arrived(a, b)
    sib.append(net.same(w.at[:, xs(2), c], net.sib))
    yield
    arrived(*sib)
    yield


def spread_y(net, view):
    rows = view(None, None, None)
    a, b = net.same(view(net.y, 0, rows), net.yp), net.same(view(net.y, 0, rows), net.ym)
    yield
    arrived(a, b)
    a = net.same(view(net.ys(-1), 0, rows // 2), net.yp)
    b = net.same(view(net.ys(1), rows // 2, rows // 2), net.ym)
    yield
    arrived(a, b)
    yield


def normed(x, gain):
    wide = x.astype(F32)
    factor = lax.rsqrt(jnp.mean(wide * wide, axis=-1, keepdims=True) + NORM_EPS)
    return (wide * factor * gain).astype(BF16)


def layer_kernel(
    tokens, attn_gain, mlp_gain, cosine, sine, first_key, s_qkv, s_out, s_gate, s_up, s_down,
    out,
    w_qkv, w_out, w_gate, w_up, w_down, xn, res, hid, q_even, q_odd, kv, vk, bias, att,
    part, result, far_a, far_b, near_p, near_m, send_sem, recv_sem, out_sem,
):
    net = Net(send_sem, recv_sem)
    x, y, z, c = net.x, net.y, net.z, net.c

    w_qkv[z, x, c] = s_qkv[...]
    for j in (0, 1):
        for w, s in ((w_gate, s_gate), (w_up, s_up), (w_down, s_down)):
            w[j, z, x, c] = s[:, j * SPAN : (j + 1) * SPAN]
    own_cols = pl.ds(pl.multiple_of(lax.rem(y, 2) * 256, 256), 256)
    own_out = w_out.at[y // 2, z, x, c, :, own_cols]
    own_out[...] = s_out[...]
    net.barrier()

    gq = gather_zx(net, w_qkv)
    go = [gather_xz(net, w_out.at[0]), gather_zx(net, w_out.at[1])]
    gg = [gather_xz(net, w_gate.at[0]), gather_zx(net, w_gate.at[1])]
    gu = [gather_xz(net, w_up.at[0]), gather_zx(net, w_up.at[1])]
    gd = [gather_xz(net, w_down.at[0]), gather_zx(net, w_down.at[1])]

    def pump(*items):
        for item in items:
            next(item, None)

    def finish(*items):
        for item in items:
            for _ in item:
                pass

    def norm_rows(src, gain, first, count):
        @pl.loop(0, count // 64)
        def _(i):
            r = pl.ds(pl.multiple_of(first + i * 64, 64), 64)
            xn[r] = normed(src[r], gain[...])

    pump(gq)
    ex = [net.send(s_out, own_out, p) for p in (net.yp, net.ym, net.y2)]
    norm_rows(tokens, attn_gain, 0, 128)
    pump(gq)
    norm_rows(tokens, attn_gain, 128, 128)
    pump(gq)
    arrived(*ex)
    pump(*go)
    norm_rows(tokens, attn_gain, 256, 128)
    pump(gq, *go)
    norm_rows(tokens, attn_gain, 384, 128)
    pump(gq, *go)
    norm_rows(tokens, attn_gain, 512, 128)
    pump(gq, *go, *gg)
    norm_rows(tokens, attn_gain, 640, 128)
    pump(gq, *go, *gg)
    pump(gq)

    def project(h):
        r = pl.ds(h * HALF, HALF)
        prod = nn(xn[r], w_qkv[...].reshape(WIDTH, 384))
        cs, sn = cosine[r], sine[r]
        lane = lax.broadcasted_iota(jnp.int32, (HALF, 128), 1)
        lead = lax.rem(lane, 64) < 32
        low = lane < 64
        for t in range(3):
            v = prod[:, t * 128 : (t + 1) * 128]
            swapped = jnp.where(lead, pltpu.roll(v, 96, 1), pltpu.roll(v, 32, 1))
            turned = v * cs + swapped * sn
            if t < 2:
                q_even[t, r] = jnp.where(low, turned, 0.0).astype(BF16)
                q_odd[t, r] = jnp.where(low, 0.0, turned).astype(BF16)
            else:
                own = jnp.where(low, turned, v)
                kv[pl.ds(ROWS + h * HALF, HALF)] = own.astype(BF16)
                vk[pl.ds(ROWS + h * HALF, HALF)] = pltpu.roll(own, 64, 1).astype(BF16)

    project(0)
    pump(*go)
    project(1)
    shift = net.send(kv.at[pl.ds(ROWS, ROWS)], kv.at[pl.ds(0, ROWS)], net.after)
    pump(*go, *gg, *gu)
    arrived(shift)
    vk[pl.ds(0, ROWS)] = pltpu.roll(kv[pl.ds(0, ROWS)].astype(F32), 64, 1).astype(BF16)

    def attend(first, count):
        @pl.loop(first, first + count)
        def _(i):
            r = pl.ds(pl.multiple_of(i * 128, 128), 128)
            keys = pl.ds(pl.multiple_of(i * 128, 128), WINDOW)
            col = lax.broadcasted_iota(jnp.int32, (128, WINDOW), 1)
            row = lax.broadcasted_iota(jnp.int32, (128, WINDOW), 0)
            lowest = first_key[r] + (ROWS - i * 128)
            allowed = (col >= lowest) & (col <= row + ROWS)
            bias[...] = jnp.where(allowed, 0.0, MASKED)
            kvw, vkw = kv[keys], vk[keys]

            def heads(q, k, v):
                s = nt(q[:, r].reshape(256, 128), k) * 0.125
                s = s + jnp.concatenate([bias[...], bias[...]], axis=0)
                e = jnp.exp(s - jnp.max(s, axis=-1, keepdims=True))
                total = jnp.sum(e, axis=-1, keepdims=True)
                return nn(e.astype(BF16), v) / total

            even = heads(q_even, kvw, vkw)
            odd = heads(q_odd, vkw, kvw)
            low = lax.broadcasted_iota(jnp.int32, (256, 128), 1) < 64
            both = jnp.where(low, even, odd).astype(BF16)
            att[y, r, pl.ds(0, 128)] = both[:128]
            att[y, r, pl.ds(128, 128)] = both[128:]

    def att_view(h):
        def view(member, first, rows):
            if member is None:
                return HALF
            return att.at[member, pl.ds(h * HALF + first, rows)]

        return view

    ga = [spread_y(net, att_view(h)) for h in (0, 1)]

    def out_project(h):
        r = pl.ds(h * HALF, HALF)

        @pl.loop(0, NZ)
        def _(k):
            cols = pl.ds(pl.multiple_of(k * 256, 256), 256)
            total = jnp.zeros((HALF, 256), F32)
            for g in range(NY):
                w = w_out[g // 2, k, :, :, :, pl.ds((g % 2) * 256, 256)].reshape(256, 256)
                total = total + nt(att[g, r], w).astype(BF16).astype(F32)
            res[r, cols] = (tokens[r, cols].astype(F32) + total).astype(BF16)

    def expand(h, j):
        r = pl.ds(h * HALF, HALF)

        @pl.loop(0, 2)
        def _(n):
            cols = pl.ds(pl.multiple_of(n * 256, 256), 256)
            gate = nn(xn[r], w_gate[j, :, :, :, :, cols].reshape(WIDTH, 256))
            up = nn(xn[r], w_up[j, :, :, :, :, cols].reshape(WIDTH, 256))
            act = gate / (1.0 + jnp.exp(-gate)) * up
            hid[j, r, cols] = act.astype(BF16)

    def contract(h, k):
        r = pl.ds(h * HALF, HALF)
        total = None
        for j in (0, 1):
            w = w_down[j, pl.ds(2 * k, 2)].reshape(SPAN, SPAN)
            term = nt(hid[j, r], w)
            total = term if total is None else total + term
        part[h * UNITS + k] = total.astype(BF16)

    def reduce_y(h, k):
        u = h * UNITS + k
        ys, p = net.ys, part.at[u]
        b2 = BLOCK // 2

        def rows(member, first, count):
            return pl.ds(pl.multiple_of(member * BLOCK + first, 16), count)

        a = net.send(p.at[rows(ys(2), 0, b2)], far_a.at[u], net.yp)
        b = net.send(p.at[rows(ys(2), b2, b2)], far_b.at[u], net.ym)
        yield
        arrived(a, b)
        ra, rb = rows(ys(1), 0, b2), rows(ys(-1), b2, b2)
        p[ra] = (p[ra].astype(F32) + far_a[u].astype(F32)).astype(BF16)
        a = net.send(p.at[rows(ys(1), 0, BLOCK)], near_p.at[u], net.yp)
        p[rb] = (p[rb].astype(F32) + far_b[u].astype(F32)).astype(BF16)
        b = net.send(p.at[rows(ys(-1), 0, BLOCK)], near_m.at[u], net.ym)
        yield
        arrived(a, b)
        own = rows(y, 0, BLOCK)
        total = p[own].astype(F32) + near_p[u].astype(F32) + near_m[u].astype(F32)
        at = pl.ds(pl.multiple_of(h * HALF + y * BLOCK, 16), BLOCK)
        result[u, own] = (res[at, pl.ds(k * SPAN, SPAN)].astype(F32) + total).astype(BF16)
        o = result.at[u]
        a, b = net.same(o.at[own], net.yp), net.same(o.at[own], net.ym)
        yield
        arrived(a, b)
        a = net.same(o.at[rows(ys(-1), 0, b2)], net.yp)
        b = net.same(o.at[rows(ys(1), b2, b2)], net.ym)
        yield
        arrived(a, b)
        stores.append(
            pltpu.make_async_copy(o, out.at[pl.ds(h * HALF, HALF), pl.ds(k * SPAN, SPAN)], out_sem.at[u])
        )
        stores[-1].start()
        yield

    stores = []
    gr = [[reduce_y(h, k) for k in range(UNITS)] for h in (0, 1)]

    attend(0, 2)
    pump(*go, *gg, *gu)
    attend(2, 1)
    pump(ga[0])
    pump(go[0], *gg, *gu)
    attend(3, 1)
    pump(*gg, *gu, *gd)
    attend(4, 1)
    pump(ga[0])
    pump(*gg, *gu, *gd)
    attend(5, 1)
    pump(ga[1])
    finish(*go)
    pump(*gg, *gu, *gd)
    pump(ga[0])
    out_project(0)
    pump(ga[1])
    finish(*gg)
    pump(*gu, *gd)
    norm_rows(res, mlp_gain, 0, HALF)
    finish(*gu)
    pump(*gd)
    expand(0, 0)
    pump(*gd)
    pump(ga[1])
    expand(0, 1)
    finish(*gd)
    for k in range(UNITS):
        contract(0, k)
        pump(gr[0][k])
    out_project(1)
    pump(gr[0][0], gr[0][1])
    norm_rows(res, mlp_gain, HALF, HALF)
    pump(gr[0][2], gr[0][3])
    expand(1, 0)
    pump(gr[0][0], gr[0][1])
    expand(1, 1)
    pump(gr[0][2], gr[0][3])
    for k in range(UNITS):
        contract(1, k)
        pump(gr[1][k], gr[0][k])
    for k in range(UNITS):
        pump(gr[1][k], gr[0][k])
    for _ in range(3):
        for k in range(UNITS):
            pump(gr[1][k])
    for s in stores:
        s.wait()
    for copy in net.copies:
        copy.wait_send()


def doc_starts(positions, doc_lengths):
    doc_ends = jnp.cumsum(doc_lengths)
    passed = doc_ends[None, :] <= positions[:, None]
    return jnp.sum(jnp.where(passed, doc_lengths[None, :], 0), axis=1)


def per_device(
    tokens, attn_gain, w_query, key_value_weight, w_out, mlp_gain, w_gate, w_up, w_down, doc_lengths
):
    base = lax.axis_index("tok") * ROWS
    positions = base + jnp.arange(ROWS, dtype=jnp.int32)
    starts = doc_starts(positions, doc_lengths)
    frequency = ROPE_BASE ** (-2.0 * jnp.arange(32, dtype=F32) / 64)
    angles = (positions - starts).astype(F32)[:, None] * frequency[None, :]
    cos, sin = jnp.cos(angles), jnp.sin(angles)
    cosine = jnp.concatenate([cos, cos, cos, cos], axis=1)
    sine = jnp.concatenate([-sin, sin, -sin, sin], axis=1)
    shard = w_query.shape[0]
    s_qkv = jnp.concatenate(
        [w_query.reshape(shard, 256), key_value_weight.reshape(shard, 128)], axis=1
    )
    args = (
        tokens, attn_gain.reshape(1, WIDTH), mlp_gain.reshape(1, WIDTH), cosine, sine,
        (starts - base)[:, None], s_qkv, w_out.reshape(256, shard).T, w_gate, w_up, w_down.T,
    )
    vmem = pl.BlockSpec(memory_space=pltpu.VMEM)
    big = (2, NZ, NX, 2, 32, SPAN)
    units = 2 * UNITS
    return pl.pallas_call(
        layer_kernel,
        out_shape=jax.ShapeDtypeStruct((ROWS, WIDTH), BF16),
        in_specs=[vmem] * len(args),
        out_specs=pl.BlockSpec(memory_space=pl.ANY),
        scratch_shapes=[
            pltpu.VMEM((NZ, NX, 2, 32, 384), BF16),
            pltpu.VMEM(big, BF16),
            pltpu.VMEM(big, BF16),
            pltpu.VMEM(big, BF16),
            pltpu.VMEM(big, BF16),
            pltpu.VMEM((ROWS, WIDTH), BF16),
            pltpu.VMEM((ROWS, WIDTH), BF16),
            pltpu.VMEM((2, ROWS, SPAN), BF16),
            pltpu.VMEM((2, ROWS, 128), BF16),
            pltpu.VMEM((2, ROWS, 128), BF16),
            pltpu.VMEM((2 * ROWS, 128), BF16),
            pltpu.VMEM((2 * ROWS, 128), BF16),
            pltpu.VMEM((128, WINDOW), F32),
            pltpu.VMEM((NY, ROWS, 256), BF16),
            pltpu.VMEM((units, HALF, SPAN), BF16),
            pltpu.VMEM((units, HALF, SPAN), BF16),
            pltpu.VMEM((units, BLOCK // 2, SPAN), BF16),
            pltpu.VMEM((units, BLOCK // 2, SPAN), BF16),
            pltpu.VMEM((units, BLOCK, SPAN), BF16),
            pltpu.VMEM((units, BLOCK, SPAN), BF16),
            pltpu.SemaphoreType.DMA((SEMS,)),
            pltpu.SemaphoreType.DMA((SEMS,)),
            pltpu.SemaphoreType.DMA((units,)),
        ],
        compiler_params=pltpu.CompilerParams(
            collective_id=0, has_side_effects=True, vmem_limit_bytes=60 * 2**20
        ),
        name="layer",
    )(*args)


def solution(mesh):
    placed = (
        P("tok", None),
        P(),
        P("tok", "fsdp", None),
        P("tok", None, "fsdp", None),
        P("fsdp", None, "tok"),
        P(),
        P("tok", "fsdp"),
        P("tok", "fsdp"),
        P("fsdp", "tok"),
        P(),
    )
    return jax.shard_map(
        per_device, mesh=mesh, in_specs=placed, out_specs=P("tok", None), check_vma=False
    )
```

```python
import jax
import jax.numpy as jnp
import numpy as np
from jax import lax
from jax.experimental import pallas as pl
from jax.experimental.pallas import tpu as pltpu
from jax.sharding import PartitionSpec as P

ROPE_BASE = 500000.0
NORM_EPS = 1e-05
MASKED = -1e30
MESH = pl.DeviceIdType.MESH
F32, BF16 = jnp.float32, jnp.bfloat16

NZ, NX, NY = 8, 4, 4
ROWS = 768
WIDTH = 2048
HALF = 384
BLOCK = 96
SPAN = 512
COLS = 256
UNITS = 8
WINDOW = 896
SEMS = 400
ROUND_Z_FIRST = ("k", "o", "g1", "u0",)
ORDER = (
    "o", "l", "q", "k", "n0", "n1", "o", "n2", "n3", "n4", "n5", "q", "g1", "k", "o", "q", "g0", "g1", "k",
    "o", "u0", "g0", "q", "g1", "k", "o", "u0", "g0", "q", "u1", "g1", "k", "u0", "d1", "o", "d0", "u1",
    "g0", "k", "d1", "q", "g1", "u0", "o", "y", "d0", "u1", "k", "d1", "o", "g0", "q", "k", "v1", "s1",
    "u0", "v0", "s0", "q", "p1", "p0", "u1", "g1", "d0", "d1", "s1", "t3", "a3", "t4", "a4", "g0", "t5",
    "a5", "y", "u0", "u1", "a3", "s0", "t0", "a0", "a4", "a5", "d0", "g1", "t1", "a1", "t2", "a2", "d1",
    "u0", "g0", "y", "g1", "a3", "u1", "u0", "a0", "g0", "a4", "a5", "d0", "y", "w1", "a0", "a1", "a2",
    "d1", "u1", "m1", "e10", "a1", "a2", "d0", "u1", "e11", "d1", "c10", "r10", "c11", "r11", "c12", "r12",
    "d0", "c13", "r13", "c14", "r14", "d1", "c15", "r15", "c16", "r16", "r10", "d0", "c17", "r11", "r12",
    "r17", "r13", "w0", "r10", "r11", "r12", "r14", "r15", "r16", "r13", "r17", "m0", "r10", "e00", "r11",
    "r12", "r14", "e01", "r15", "r13", "r16", "c00", "r00", "r17", "r10", "c01", "r01", "r11", "c02", "r02",
    "r12", "c03", "r03", "c04", "r04", "r14", "c05", "r05", "c06", "r06", "r15", "c07", "r07", "r13", "r16",
    "r00", "r17", "r01", "r02", "r03", "r04", "r14", "r05", "r06", "r15", "r07", "r16", "r00", "r17", "r01",
    "r02", "r03", "r04", "r05", "r06", "r07", "r00", "r01", "r02", "r03", "r04", "r05", "r06", "r07", "r00",
    "r01", "r02", "r03", "r04", "r05", "r06", "r07",
)


def nt(a, b):
    return lax.dot_general(a, b, (((1,), (1,)), ((), ())), preferred_element_type=F32)


def nn(a, b):
    return jnp.dot(a, b, preferred_element_type=F32)


class Net:
    def __init__(self, send_sem, recv_sem):
        tok, self.y = lax.axis_index("tok"), lax.axis_index("fsdp")
        self.c = lax.rem(tok, 2)
        self.x = lax.rem(tok // 2, NX)
        self.z = tok // (2 * NX)
        self.send_sem, self.recv_sem = send_sem, recv_sem
        self.copies = []
        z, x, c, y = self.z, self.x, self.c, self.y

        def at(z, x, c):
            return (z * NX + x) * 2 + c

        self.zp = (at(self.zs(1), x, c), y)
        self.zm = (at(self.zs(-1), x, c), y)
        self.xp = (at(z, self.xs(1), c), y)
        self.xm = (at(z, self.xs(-1), c), y)
        self.sib = (at(z, x, 1 - c), y)
        self.yp = (tok, self.ys(1))
        self.ym = (tok, self.ys(-1))
        self.y2 = (tok, self.ys(2))
        count = 2 * NX * NZ
        self.after = (lax.rem(tok + 1, count), y)
        self.before = (lax.rem(tok + count - 1, count), y)

    def zs(self, d):
        return lax.rem(self.z + NZ + d, NZ)

    def xs(self, d):
        return lax.rem(self.x + NX + d, NX)

    def ys(self, d):
        return lax.rem(self.y + NY + d, NY)

    def enter(self):
        self.partners = [
            self.zp, self.zm, self.xp, self.xm, self.sib,
            self.yp, self.ym, self.y2, self.after, self.before,
        ]
        sem = pltpu.get_barrier_semaphore()
        for p in self.partners:
            pl.semaphore_signal(sem, 1, device_id=p, device_id_type=MESH)

    def entered(self):
        pl.semaphore_wait(pltpu.get_barrier_semaphore(), len(self.partners))

    def send(self, src, dst, to):
        i = len(self.copies)
        copy = pltpu.make_async_remote_copy(
            src_ref=src, dst_ref=dst, send_sem=self.send_sem.at[i],
            recv_sem=self.recv_sem.at[i], device_id=to, device_id_type=MESH,
        )
        copy.start()
        self.copies.append(copy)
        return copy

    def same(self, ref, to):
        return self.send(ref, ref, to)


def arrived(*copies):
    for copy in copies:
        copy.wait_recv()


def gather_xz(net, w):
    x, z, c, xs, zs = net.x, net.z, net.c, net.xs, net.zs
    a, b = net.same(w.at[z, x, c], net.xp), net.same(w.at[z, x, c], net.xm)
    yield
    arrived(a, b)
    a = net.same(w.at[z, xs(-1), c, pl.ds(0, 16)], net.xp)
    b = net.same(w.at[z, xs(1), c, pl.ds(16, 16)], net.xm)
    yield
    arrived(a, b)
    own = w.at[z, :, c]
    a, b, sib = net.same(own, net.zp), net.same(own, net.zm), [net.same(own, net.sib)]
    yield
    for hop in (1, 2):
        arrived(a, b, *sib)
        lo, hi = w.at[zs(-hop), :, c], w.at[zs(hop), :, c]
        a, b = net.same(lo, net.zp), net.same(hi, net.zm)
        sib = [net.same(lo, net.sib), net.same(hi, net.sib)]
        yield
    arrived(a, b, *sib)
    a = net.same(w.at[zs(-3), pl.ds(0, 2), c], net.zp)
    b = net.same(w.at[zs(3), pl.ds(2, 2), c], net.zm)
    sib = [net.same(w.at[zs(-3), :, c], net.sib), net.same(w.at[zs(3), :, c], net.sib)]
    yield
    arrived(a, b, *sib)
    last = net.same(w.at[zs(4), :, c], net.sib)
    yield
    arrived(last)
    yield


def gather_zx(net, w):
    x, z, c, xs, zs = net.x, net.z, net.c, net.xs, net.zs
    a, b = net.same(w.at[z, x, c], net.zp), net.same(w.at[z, x, c], net.zm)
    yield
    for hop in (1, 2):
        arrived(a, b)
        a, b = net.same(w.at[zs(-hop), x, c], net.zp), net.same(w.at[zs(hop), x, c], net.zm)
        yield
    arrived(a, b)
    a = net.same(w.at[zs(-3), x, c, pl.ds(0, 16)], net.zp)
    b = net.same(w.at[zs(3), x, c, pl.ds(16, 16)], net.zm)
    yield
    arrived(a, b)
    a, b = net.same(w.at[:, x, c], net.xp), net.same(w.at[:, x, c], net.xm)
    sib = [net.same(w.at[:, x, c], net.sib)]
    yield
    arrived(a, b)
    lo, hi = xs(-1), xs(1)
    a = net.same(w.at[pl.ds(0, 4), lo, c], net.xp)
    b = net.same(w.at[pl.ds(4, 4), hi, c], net.xm)
    sib += [net.same(w.at[:, lo, c], net.sib), net.same(w.at[:, hi, c], net.sib)]
    yield
    arrived(a, b)
    sib.append(net.same(w.at[:, xs(2), c], net.sib))
    yield
    arrived(*sib)
    yield


def spread_y(net, view):
    rows = view(None, None, None)
    a, b = net.same(view(net.y, 0, rows), net.yp), net.same(view(net.y, 0, rows), net.ym)
    yield
    arrived(a, b)
    a = net.same(view(net.ys(-1), 0, rows // 2), net.yp)
    b = net.same(view(net.ys(1), rows // 2, rows // 2), net.ym)
    yield
    arrived(a, b)
    yield


def normed(x, gain):
    wide = x.astype(F32)
    factor = lax.rsqrt(jnp.mean(wide * wide, axis=-1, keepdims=True) + NORM_EPS)
    return (wide * factor * gain).astype(BF16)


def rope_table():
    f = np.float32(ROPE_BASE) ** (np.float32(-2.0) * np.arange(32, dtype=np.float32) / np.float32(64))
    angle = np.arange(ROWS, dtype=np.float32)[:, None] * f.astype(np.float32)[None, :]
    cos, sin = np.cos(angle.astype(np.float64)), np.sin(angle.astype(np.float64))
    left = np.concatenate([cos, cos, cos, cos, -sin, sin, -sin, sin], axis=1).astype(np.float32)
    terms = []
    for _ in range(3):
        terms.append(left.astype(BF16))
        left = left - terms[-1].astype(np.float32)
    return np.concatenate(terms, axis=1)


def layer_kernel(
    tokens, attn_gain, mlp_gain, lengths, table, s_query, s_pair, s_out, s_gate, s_up, s_down,
    out,
    w_q, w_kv, w_out, w_gate, w_up, w_down, xn, res, hid, q_even, q_odd, kv, vk, bias, att,
    part, far_a, far_b, near_p, near_m, cosine, sine, first_key, send_sem, recv_sem,
):
    net = Net(send_sem, recv_sem)
    x, y, z, c = net.x, net.y, net.z, net.c
    net.enter()

    w_kv[z, x, c] = jnp.concatenate([s_pair[:, i, :] for i in range(2)], axis=1)
    w_q[z, x, c] = jnp.concatenate([s_query[:, h, :] for h in range(4)], axis=1)
    w_out[y, z, x, c] = jnp.concatenate([s_out[h] for h in range(4)], axis=1)
    for j in (0, 1):
        w_gate[j, z, x, c] = s_gate[:, j * SPAN : (j + 1) * SPAN]
        w_up[j, z, x, c] = s_up[:, j * SPAN : (j + 1) * SPAN]
        w_down[j, z, x, c] = s_down[:, j * SPAN : (j + 1) * SPAN]
    net.entered()

    def spread_out():
        ys = net.ys

        def half(member, first):
            return w_out.at[member, pl.ds(first, 4), :, net.c]

        def whole(member):
            return w_out.at[member, :, :, net.c]

        a, b = net.same(whole(y), net.yp), net.same(whole(y), net.ym)
        yield
        arrived(a, b)
        a, b = net.same(half(ys(-1), 0), net.yp), net.same(half(ys(1), 4), net.ym)
        sib = [net.same(whole(ys(-1)), net.sib), net.same(whole(ys(1)), net.sib)]
        yield
        arrived(a, b)
        sib.append(net.same(whole(ys(2)), net.sib))
        yield
        arrived(*sib)
        yield

    def norm_rows(src, gain, first, count):
        @pl.loop(0, count // 64)
        def _(i):
            r = pl.ds(pl.multiple_of(first + i * 64, 64), 64)
            xn[r] = normed(src[r], gain[...])

    def rope():
        length = lengths[...].astype(F32)
        across = lax.broadcasted_iota(jnp.int32, (256, 256), 1)
        down = lax.broadcasted_iota(jnp.int32, (256, 256), 0)
        column = jnp.sum(jnp.where(across == down, length, 0.0), axis=1, keepdims=True)
        ends = jnp.sum(jnp.where(down <= across, column, 0.0), axis=0, keepdims=True)
        base = ((z * NX + x) * 2 + c) * ROWS
        local = lax.broadcasted_iota(jnp.int32, (ROWS, 1), 0)
        start = jnp.sum(
            jnp.where(ends <= (base + local).astype(F32), length, 0.0), axis=1, keepdims=True
        )
        begin = start.astype(jnp.int32) - base
        first_key[...] = begin
        onehot = (lax.broadcasted_iota(jnp.int32, (ROWS, ROWS), 1) == local - begin).astype(F32)
        turn = nn(onehot.astype(BF16), table[...])
        turn = turn[:, :256] + turn[:, 256:512] + turn[:, 512:]
        cosine[...] = turn[:, :128]
        sine[...] = turn[:, 128:]

    def turned(v, r):
        lead = lax.rem(lax.broadcasted_iota(jnp.int32, (HALF, 128), 1), 64) < 32
        swapped = jnp.where(lead, pltpu.roll(v, 96, 1), pltpu.roll(v, 32, 1))
        return v * cosine[r] + swapped * sine[r]

    def project_pair(h):
        r, there = pl.ds(h * HALF, HALF), pl.ds(ROWS + h * HALF, HALF)
        low = lax.broadcasted_iota(jnp.int32, (HALF, 128), 1) < 64
        prod = nn(xn[r], w_kv[...].reshape(WIDTH, 128))
        own = jnp.where(low, turned(prod, r), prod)
        kv[there] = own.astype(BF16)
        vk[there] = pltpu.roll(own, 64, 1).astype(BF16)

    def project_query(h):
        r = pl.ds(h * HALF, HALF)
        low = lax.broadcasted_iota(jnp.int32, (HALF, 128), 1) < 64
        prod = nn(xn[r], w_q[...].reshape(WIDTH, 256))
        for t in range(2):
            v = turned(prod[:, t * 128 : (t + 1) * 128], r)
            q_even[t, r] = jnp.where(low, v, 0.0).astype(BF16)
            q_odd[t, r] = jnp.where(low, 0.0, v).astype(BF16)

    def shift(h):
        there = pl.ds(h * HALF, HALF)
        copy = net.send(kv.at[pl.ds(ROWS + h * HALF, HALF)], kv.at[there], net.after)
        yield
        arrived(copy)
        vk[there] = pltpu.roll(kv[there].astype(F32), 64, 1).astype(BF16)
        yield

    def attend(i):
        r = pl.ds(i * 128, 128)
        keys = pl.ds(i * 128, WINDOW)
        col = lax.broadcasted_iota(jnp.int32, (128, WINDOW), 1)
        row = lax.broadcasted_iota(jnp.int32, (128, WINDOW), 0)
        lowest = first_key[r] + (ROWS - i * 128)
        allowed = (col >= lowest) & (col <= row + ROWS)
        bias[...] = jnp.where(allowed, 0.0, MASKED)
        kvw, vkw = kv[keys], vk[keys]

        def heads(q, k, v):
            s = nt(q[:, r].reshape(256, 128), k) * 0.125
            s = s + jnp.concatenate([bias[...], bias[...]], axis=0)
            e = jnp.exp(s - jnp.max(s, axis=-1, keepdims=True))
            total = jnp.sum(e, axis=-1, keepdims=True)
            return nn(e.astype(BF16), v) / total

        even = heads(q_even, kvw, vkw)
        odd = heads(q_odd, vkw, kvw)
        low = lax.broadcasted_iota(jnp.int32, (256, 128), 1) < 64
        both = jnp.where(low, even, odd).astype(BF16)
        att[y, r, pl.ds(0, 128)] = both[:128]
        att[y, r, pl.ds(128, 128)] = both[128:]

    def att_view(i):
        def view(member, first, rows):
            if member is None:
                return 128
            return att.at[member, pl.ds(i * 128 + first, rows)]

        return view

    def out_project(h):
        r = pl.ds(h * HALF, HALF)

        @pl.loop(0, NZ)
        def _(k):
            cols = pl.ds(pl.multiple_of(k * 256, 256), 256)
            total = jnp.zeros((HALF, 256), F32)
            for g in range(NY):
                w = w_out[g, k].reshape(256, 256)
                total = total + nt(att[g, r], w).astype(BF16).astype(F32)
            res[r, cols] = (tokens[r, cols].astype(F32) + total).astype(BF16)

    def expand(h, j):
        r = pl.ds(h * HALF, HALF)

        @pl.loop(0, 2)
        def _(n):
            cols = pl.ds(pl.multiple_of(n * 256, 256), 256)
            gate = nn(xn[r], w_gate[j, :, :, :, :, cols].reshape(WIDTH, 256))
            up = nn(xn[r], w_up[j, :, :, :, :, cols].reshape(WIDTH, 256))
            act = gate / (1.0 + jnp.exp(-gate)) * up
            hid[j, r, cols] = act.astype(BF16)

    def place(k):
        return net.zs((0, -1, 1, -2, 2, -3, 3, 4)[k])

    def contract(h, k):
        r = pl.ds(h * HALF, HALF)
        total = None
        for j in (0, 1):
            term = nt(hid[j, r], w_down[j, place(k)].reshape(COLS, SPAN))
            total = term if total is None else total + term
        part[h * UNITS + k] = total.astype(BF16)

    def reduce_y(h, k):
        u = h * UNITS + k
        ys, p = net.ys, part.at[u]
        b2 = BLOCK // 2
        cols = pl.ds(pl.multiple_of(place(k) * COLS, COLS), COLS)

        def rows(member, first, count):
            return pl.ds(pl.multiple_of(member * BLOCK + first, 16), count)

        a = net.send(p.at[rows(ys(2), 0, b2)], far_a.at[u], net.yp)
        b = net.send(p.at[rows(ys(2), b2, b2)], far_b.at[u], net.ym)
        yield
        arrived(a, b)
        ra, rb = rows(ys(1), 0, b2), rows(ys(-1), b2, b2)
        p[ra] = (p[ra].astype(F32) + far_a[u].astype(F32)).astype(BF16)
        a = net.send(p.at[rows(ys(1), 0, BLOCK)], near_p.at[u], net.yp)
        p[rb] = (p[rb].astype(F32) + far_b[u].astype(F32)).astype(BF16)
        b = net.send(p.at[rows(ys(-1), 0, BLOCK)], near_m.at[u], net.ym)
        yield
        arrived(a, b)
        own = rows(y, 0, BLOCK)
        total = p[own].astype(F32) + near_p[u].astype(F32) + near_m[u].astype(F32)

        def there(member, first, count):
            return out.at[pl.ds(pl.multiple_of(h * HALF + member * BLOCK + first, 16), count), cols]

        at = pl.ds(pl.multiple_of(h * HALF + y * BLOCK, 16), BLOCK)
        out[at, cols] = (res[at, cols].astype(F32) + total).astype(BF16)
        mine = there(y, 0, BLOCK)
        a, b = net.same(mine, net.yp), net.same(mine, net.ym)
        yield
        arrived(a, b)
        a, b = net.same(there(ys(-1), 0, b2), net.yp), net.same(there(ys(1), b2, b2), net.ym)
        yield
        arrived(a, b)
        yield

    routes = dict(
        q=w_q, k=w_kv, o=w_out.at[y], g0=w_gate.at[0], g1=w_gate.at[1],
        u0=w_up.at[0], u1=w_up.at[1], d0=w_down.at[0], d1=w_down.at[1],
    )
    moves = {n: (gather_zx if n in ROUND_Z_FIRST else gather_xz)(net, w) for n, w in routes.items()}
    moves["y"] = spread_out()
    moves.update({"s%d" % h: shift(h) for h in (0, 1)})
    moves.update({"a%d" % i: spread_y(net, att_view(i)) for i in range(6)})
    moves.update({"r%d%d" % (h, k): reduce_y(h, k) for h in (0, 1) for k in range(UNITS)})
    work = {
        "n": lambda i: norm_rows(tokens, attn_gain, i * 128, 128),
        "l": rope,
        "v": project_pair,
        "p": project_query,
        "t": attend,
        "w": out_project,
        "m": lambda h: norm_rows(res, mlp_gain, h * HALF, HALF),
        "e": expand,
        "c": contract,
    }
    for step in ORDER:
        if step in moves:
            next(moves[step])
        else:
            work[step[0]](*(int(digit) for digit in step[1:]))
    for copy in net.copies:
        copy.wait_send()


def per_device(
    tokens, attn_gain, w_query, key_value_weight, w_out, mlp_gain, w_gate, w_up, w_down, doc_lengths
):
    shard = w_query.shape[0]
    args = (
        tokens, attn_gain.reshape(1, WIDTH), mlp_gain.reshape(1, WIDTH), doc_lengths.reshape(1, -1),
        jnp.asarray(rope_table()), w_query, key_value_weight.reshape(shard, 2, 64), jnp.swapaxes(w_out, 1, 2),
        w_gate, w_up, w_down.T,
    )
    vmem = pl.BlockSpec(memory_space=pltpu.VMEM)
    big = (2, NZ, NX, 2, 32, SPAN)
    units = 2 * UNITS
    return pl.pallas_call(
        layer_kernel,
        out_shape=pltpu.VMEM((ROWS, WIDTH), BF16),
        in_specs=[vmem] * len(args),
        out_specs=vmem,
        scratch_shapes=[
            pltpu.VMEM((NZ, NX, 2, 32, 256), BF16),
            pltpu.VMEM((NZ, NX, 2, 32, 128), BF16),
            pltpu.VMEM((NY, NZ, NX, 2, 32, 256), BF16),
            pltpu.VMEM(big, BF16),
            pltpu.VMEM(big, BF16),
            pltpu.VMEM(big, BF16),
            pltpu.VMEM((ROWS, WIDTH), BF16),
            pltpu.VMEM((ROWS, WIDTH), BF16),
            pltpu.VMEM((2, ROWS, SPAN), BF16),
            pltpu.VMEM((2, ROWS, 128), BF16),
            pltpu.VMEM((2, ROWS, 128), BF16),
            pltpu.VMEM((2 * ROWS, 128), BF16),
            pltpu.VMEM((2 * ROWS, 128), BF16),
            pltpu.VMEM((128, WINDOW), F32),
            pltpu.VMEM((NY, ROWS, 256), BF16),
            pltpu.VMEM((units, HALF, COLS), BF16),
            pltpu.VMEM((units, BLOCK // 2, COLS), BF16),
            pltpu.VMEM((units, BLOCK // 2, COLS), BF16),
            pltpu.VMEM((units, BLOCK, COLS), BF16),
            pltpu.VMEM((units, BLOCK, COLS), BF16),
            pltpu.VMEM((ROWS, 128), F32),
            pltpu.VMEM((ROWS, 128), F32),
            pltpu.VMEM((ROWS, 1), jnp.int32),
            pltpu.SemaphoreType.DMA((SEMS,)),
            pltpu.SemaphoreType.DMA((SEMS,)),
        ],
        compiler_params=pltpu.CompilerParams(
            collective_id=0, has_side_effects=True, vmem_limit_bytes=56 * 2**20
        ),
        name="layer",
    )(*args)


def solution(mesh):
    placed = (
        P("tok", None),
        P(),
        P("tok", "fsdp", None),
        P("tok", None, "fsdp", None),
        P("fsdp", None, "tok"),
        P(),
        P("tok", "fsdp"),
        P("tok", "fsdp"),
        P("fsdp", "tok"),
        P(),
    )
    return jax.shard_map(
        per_device, mesh=mesh, in_specs=placed, out_specs=P("tok", None), check_vma=False
    )
```

```python
import jax
import jax.numpy as jnp
import numpy as np
from jax import lax
from jax.experimental import pallas as pl
from jax.experimental.pallas import tpu as pltpu
from jax.sharding import PartitionSpec as P

ROPE_BASE = 500000.0
NORM_EPS = 1e-05
MASKED = -1e30
MESH = pl.DeviceIdType.MESH
F32, BF16 = jnp.float32, jnp.bfloat16

NZ, NX, NY = 8, 4, 4
ROWS = 768
WIDTH = 2048
HALF = 384
BLOCK = 96
SPAN = 512
COLS = 256
UNITS = 8
WINDOW = 896
SENDS, SLOTS = 96, 203
FIRST = ("k", "q")
LATER = ("o", "y", "g0", "g1", "u0", "u1")
SPREAD_DIRECT = True
DIRECT = ("k", "o",)
ROUND_Z_FIRST = ("q", "g0", "u1",)
ORDER = (
    "o", "q", "l", "g0", "n0", "k", "n1", "n2", "n3", "q", "o", "n4", "n5", "g0", "k", "u0", "q", "g1",
    "u1", "u0", "o", "g0", "g1", "k", "q", "u1", "u0", "g1", "o", "y", "g0", "d1", "q", "k", "u1", "o",
    "d0", "k", "v1", "s1", "d1", "u0", "v0", "s0", "q", "g1", "g0", "d0", "u1", "d1", "s1", "s0", "u0", "q",
    "y", "g1", "u1", "q", "p1", "p0", "t3", "a3", "g0", "d1", "d0", "t4", "a4", "u0", "t5", "a5", "g1", "y",
    "t0", "a0", "u1", "t1", "a1", "a3", "g0", "d1", "t2", "a2", "a4", "y", "d0", "u0", "u1", "g1", "g0",
    "a5", "w1", "a0", "u1", "g1", "d1", "u0", "m1", "d0", "a1", "e10", "e11", "a2", "d1", "c10", "r10",
    "c11", "r11", "c12", "r12", "d0", "c13", "r13", "c14", "r14", "d1", "w0", "r10", "r11", "r12", "r13",
    "r14", "d0", "c15", "r15", "c16", "r16", "m0", "e00", "r10", "r11", "r12", "r13", "d0", "c17", "r17",
    "r14", "r15", "r16", "e01", "r10", "r11", "c00", "r00", "r12", "c01", "r01", "c02", "r02", "r13", "c03",
    "r03", "r17", "c04", "r04", "r14", "c05", "r05", "c06", "r06", "r15", "c07", "r07", "r16", "r10", "r11",
    "r00", "r12", "r01", "r02", "r13", "r03", "r17", "r04", "r14", "r05", "r06", "r15", "r07", "r16", "r00",
    "r01", "r02", "r03", "r17", "r04", "r05", "r06", "r15", "r07", "r16", "r00", "r01", "r02", "r03", "r17",
    "r04", "r05", "r06", "r07", "r00", "r01", "r02", "r03", "r04", "r05", "r06", "r07",
)


def nt(a, b):
    return lax.dot_general(a, b, (((1,), (1,)), ((), ())), preferred_element_type=F32)


def nn(a, b):
    return jnp.dot(a, b, preferred_element_type=F32)


class Net:
    def __init__(self, send_sem, recv_sem):
        tok, self.y = lax.axis_index("tok"), lax.axis_index("fsdp")
        self.c = lax.rem(tok, 2)
        self.x = lax.rem(tok // 2, NX)
        self.z = tok // (2 * NX)
        self.send_sem, self.recv_sem = send_sem, recv_sem
        self.copies = []
        self.step, self.slots, self.used = None, 0, {}
        z, x, c, y = self.z, self.x, self.c, self.y

        def at(z, x, c):
            return (z * NX + x) * 2 + c

        self.zp = (at(self.zs(1), x, c), y)
        self.zm = (at(self.zs(-1), x, c), y)
        self.xp = (at(z, self.xs(1), c), y)
        self.xm = (at(z, self.xs(-1), c), y)
        self.sib = (at(z, x, 1 - c), y)
        self.z2p = (at(self.zs(2), x, c), y)
        self.z2m = (at(self.zs(-2), x, c), y)
        self.x2 = (at(z, self.xs(2), c), y)
        self.yp = (tok, self.ys(1))
        self.ym = (tok, self.ys(-1))
        self.y2 = (tok, self.ys(2))
        count = 2 * NX * NZ
        self.after = (lax.rem(tok + 1, count), y)
        self.before = (lax.rem(tok + count - 1, count), y)

    def zs(self, d):
        return lax.rem(self.z + NZ + d, NZ)

    def xs(self, d):
        return lax.rem(self.x + NX + d, NX)

    def ys(self, d):
        return lax.rem(self.y + NY + d, NY)

    def enter(self):
        self.partners = [
            self.zp, self.zm, self.xp, self.xm, self.sib, self.z2p, self.z2m, self.x2,
            self.yp, self.ym, self.y2, self.after, self.before,
        ]
        sem = pltpu.get_barrier_semaphore()
        for p in self.partners:
            pl.semaphore_signal(sem, 1, device_id=p, device_id_type=MESH)

    def entered(self):
        pl.semaphore_wait(pltpu.get_barrier_semaphore(), len(self.partners))

    def send(self, src, dst, to, again=()):
        i = len(self.copies)
        if i >= SENDS:
            self.copies[i - SENDS].wait_send()
        free = [n for n in again if self.used.get(n)]
        if free:
            slot = self.used[free[0]].pop()
        else:
            slot = self.slots
            self.slots += 1
            if not again:
                self.used.setdefault(self.step, []).append(slot)
        copy = pltpu.make_async_remote_copy(
            src_ref=src, dst_ref=dst, send_sem=self.send_sem.at[i % SENDS],
            recv_sem=self.recv_sem.at[slot], device_id=to, device_id_type=MESH,
        )
        copy.start()
        self.copies.append(copy)
        return copy

    def same(self, ref, to, again=()):
        return self.send(ref, ref, to, again)


def arrived(*copies):
    for copy in copies:
        copy.wait_recv()


def gather_xz(net, w):
    x, z, c, xs, zs = net.x, net.z, net.c, net.xs, net.zs
    a, b = net.same(w.at[z, x, c], net.xp), net.same(w.at[z, x, c], net.xm)
    yield
    arrived(a, b)
    a = net.same(w.at[z, xs(-1), c, pl.ds(0, 16)], net.xp)
    b = net.same(w.at[z, xs(1), c, pl.ds(16, 16)], net.xm)
    yield
    arrived(a, b)
    own = w.at[z, :, c]
    a, b, sib = net.same(own, net.zp), net.same(own, net.zm), [net.same(own, net.sib)]
    yield
    for hop in (1, 2):
        arrived(a, b, *sib)
        lo, hi = w.at[zs(-hop), :, c], w.at[zs(hop), :, c]
        a, b = net.same(lo, net.zp), net.same(hi, net.zm)
        sib = [net.same(lo, net.sib), net.same(hi, net.sib)]
        yield
    arrived(a, b, *sib)
    a = net.same(w.at[zs(-3), pl.ds(0, 2), c], net.zp)
    b = net.same(w.at[zs(3), pl.ds(2, 2), c], net.zm)
    sib = [net.same(w.at[zs(-3), :, c], net.sib), net.same(w.at[zs(3), :, c], net.sib)]
    yield
    arrived(a, b, *sib)
    last = net.same(w.at[zs(4), :, c], net.sib)
    yield
    arrived(last)
    yield


def gather_zx(net, w):
    x, z, c, xs, zs = net.x, net.z, net.c, net.xs, net.zs
    a, b = net.same(w.at[z, x, c], net.zp), net.same(w.at[z, x, c], net.zm)
    yield
    for hop in (1, 2):
        arrived(a, b)
        a, b = net.same(w.at[zs(-hop), x, c], net.zp), net.same(w.at[zs(hop), x, c], net.zm)
        yield
    arrived(a, b)
    a = net.same(w.at[zs(-3), x, c, pl.ds(0, 16)], net.zp)
    b = net.same(w.at[zs(3), x, c, pl.ds(16, 16)], net.zm)
    yield
    arrived(a, b)
    a, b = net.same(w.at[:, x, c], net.xp), net.same(w.at[:, x, c], net.xm)
    sib = [net.same(w.at[:, x, c], net.sib)]
    yield
    arrived(a, b)
    lo, hi = xs(-1), xs(1)
    a = net.same(w.at[pl.ds(0, 4), lo, c], net.xp)
    b = net.same(w.at[pl.ds(4, 4), hi, c], net.xm)
    sib += [net.same(w.at[:, lo, c], net.sib), net.same(w.at[:, hi, c], net.sib)]
    yield
    arrived(a, b)
    sib.append(net.same(w.at[:, xs(2), c], net.sib))
    yield
    arrived(*sib)
    yield


def gather_direct(net, w):
    x, z, c, xs, zs = net.x, net.z, net.c, net.xs, net.zs
    own = w.at[z, x, c]
    got = [net.same(own, p) for p in (net.xp, net.xm, net.x2)]
    yield
    arrived(*got)
    own = w.at[z, :, c]
    got = [net.same(own, p) for p in (net.zp, net.zm, net.z2p, net.z2m)]
    sib = [net.same(own, net.sib)]
    yield
    arrived(*got)
    lo, hi = w.at[zs(-2), :, c], w.at[zs(2), :, c]
    got = [
        net.same(lo, net.zp),
        net.same(hi, net.zm),
        net.same(w.at[zs(-2), pl.ds(0, 2), c], net.z2p),
        net.same(w.at[zs(2), pl.ds(2, 2), c], net.z2m),
    ]
    sib += [net.same(w.at[zs(d), :, c], net.sib) for d in (-2, -1, 1, 2)]
    yield
    arrived(*got)
    sib += [net.same(w.at[zs(d), :, c], net.sib) for d in (-3, 3, 4)]
    yield
    arrived(*sib)
    yield


def spread_y(net, view):
    rows = view(None, None, None)
    own = view(net.y, 0, rows)
    if SPREAD_DIRECT:
        got = [net.same(own, p) for p in (net.yp, net.ym, net.y2)]
        yield
        arrived(*got)
        yield
        return
    a, b = net.same(own, net.yp), net.same(own, net.ym)
    yield
    arrived(a, b)
    a = net.same(view(net.ys(-1), 0, rows // 2), net.yp)
    b = net.same(view(net.ys(1), rows // 2, rows // 2), net.ym)
    yield
    arrived(a, b)
    yield


def normed(x, gain):
    wide = x.astype(F32)
    factor = lax.rsqrt(jnp.mean(wide * wide, axis=-1, keepdims=True) + NORM_EPS)
    return (wide * factor * gain).astype(BF16)


def rope_table():
    f = np.float32(ROPE_BASE) ** (np.float32(-2.0) * np.arange(32, dtype=np.float32) / np.float32(64))
    angle = np.arange(ROWS, dtype=np.float32)[:, None] * f.astype(np.float32)[None, :]
    cos, sin = np.cos(angle.astype(np.float64)), np.sin(angle.astype(np.float64))
    left = np.concatenate([cos, cos, cos, cos, -sin, sin, -sin, sin], axis=1).astype(np.float32)
    terms = []
    for _ in range(3):
        terms.append(left.astype(BF16))
        left = left - terms[-1].astype(np.float32)
    return np.concatenate(terms, axis=1)


def layer_kernel(
    tokens_hbm, attn_gain, mlp_gain, lengths, table_hbm, s_query, s_pair, s_out, s_gate, s_up, s_down,
    out,
    w_q, w_kv, w_out, w_gate, w_up, w_down, xn, res, hid, q_even, q_odd, kv, vk, bias, att,
    part, far_a, far_b, near_p, near_m, cosine, sine, first_key, tokens, table, send_sem, recv_sem,
    own_sem,
):
    net = Net(send_sem, recv_sem)
    x, y, z, c = net.x, net.y, net.z, net.c
    net.enter()
    shards = [
        (s.at[:, pl.ds(j * SPAN, SPAN)], w.at[j, z, x, c])
        for w, s in ((w_gate, s_gate), (w_up, s_up), (w_down, s_down))
        for j in (0, 1)
    ]
    own = [
        pltpu.make_async_copy(src, dst, own_sem.at[i])
        for i, (src, dst) in enumerate([(tokens_hbm, tokens), (table_hbm, table)] + shards)
    ]
    for copy in own:
        copy.start()

    w_kv[z, x, c] = jnp.concatenate([s_pair[:, i, :] for i in range(2)], axis=1)
    w_q[z, x, c] = jnp.concatenate([s_query[:, h, :] for h in range(4)], axis=1)
    w_out[y, z, x, c] = jnp.concatenate([s_out[h] for h in range(4)], axis=1)
    for copy in own[2:]:
        copy.wait()
    net.entered()

    def spread_out():
        ys = net.ys

        def half(member, first):
            return w_out.at[member, pl.ds(first, 4), :, net.c]

        def whole(member):
            return w_out.at[member, :, :, net.c]

        a, b = net.same(whole(y), net.yp), net.same(whole(y), net.ym)
        yield
        arrived(a, b)
        a, b = net.same(half(ys(-1), 0), net.yp), net.same(half(ys(1), 4), net.ym)
        sib = [net.same(whole(ys(-1)), net.sib), net.same(whole(ys(1)), net.sib)]
        yield
        arrived(a, b)
        sib.append(net.same(whole(ys(2)), net.sib))
        yield
        arrived(*sib)
        yield

    def norm_rows(src, gain, first, count):
        if src is tokens and first == 0:
            own[0].wait()

        @pl.loop(0, count // 64)
        def _(i):
            r = pl.ds(pl.multiple_of(first + i * 64, 64), 64)
            xn[r] = normed(src[r], gain[...])

    def rope():
        own[1].wait()
        length = lengths[...].astype(F32)
        across = lax.broadcasted_iota(jnp.int32, (256, 256), 1)
        down = lax.broadcasted_iota(jnp.int32, (256, 256), 0)
        column = jnp.sum(jnp.where(across == down, length, 0.0), axis=1, keepdims=True)
        ends = jnp.sum(jnp.where(down <= across, column, 0.0), axis=0, keepdims=True)
        base = ((z * NX + x) * 2 + c) * ROWS
        local = lax.broadcasted_iota(jnp.int32, (ROWS, 1), 0)
        start = jnp.sum(
            jnp.where(ends <= (base + local).astype(F32), length, 0.0), axis=1, keepdims=True
        )
        begin = start.astype(jnp.int32) - base
        first_key[...] = begin
        onehot = (lax.broadcasted_iota(jnp.int32, (ROWS, ROWS), 1) == local - begin).astype(F32)
        turn = nn(onehot.astype(BF16), table[...])
        turn = turn[:, :256] + turn[:, 256:512] + turn[:, 512:]
        cosine[...] = turn[:, :128]
        sine[...] = turn[:, 128:]

    def turned(v, r):
        lead = lax.rem(lax.broadcasted_iota(jnp.int32, (HALF, 128), 1), 64) < 32
        swapped = jnp.where(lead, pltpu.roll(v, 96, 1), pltpu.roll(v, 32, 1))
        return v * cosine[r] + swapped * sine[r]

    def project_pair(h):
        r, there = pl.ds(h * HALF, HALF), pl.ds(ROWS + h * HALF, HALF)
        low = lax.broadcasted_iota(jnp.int32, (HALF, 128), 1) < 64
        prod = nn(xn[r], w_kv[...].reshape(WIDTH, 128))
        own = jnp.where(low, turned(prod, r), prod)
        kv[there] = own.astype(BF16)
        vk[there] = pltpu.roll(own, 64, 1).astype(BF16)

    def project_query(h):
        r = pl.ds(h * HALF, HALF)
        low = lax.broadcasted_iota(jnp.int32, (HALF, 128), 1) < 64
        prod = nn(xn[r], w_q[...].reshape(WIDTH, 256))
        for t in range(2):
            v = turned(prod[:, t * 128 : (t + 1) * 128], r)
            q_even[t, r] = jnp.where(low, v, 0.0).astype(BF16)
            q_odd[t, r] = jnp.where(low, 0.0, v).astype(BF16)

    def shift(h):
        there = pl.ds(h * HALF, HALF)
        copy = net.send(kv.at[pl.ds(ROWS + h * HALF, HALF)], kv.at[there], net.after)
        yield
        arrived(copy)
        vk[there] = pltpu.roll(kv[there].astype(F32), 64, 1).astype(BF16)
        yield

    def attend(i):
        r = pl.ds(i * 128, 128)
        keys = pl.ds(i * 128, WINDOW)
        col = lax.broadcasted_iota(jnp.int32, (128, WINDOW), 1)
        row = lax.broadcasted_iota(jnp.int32, (128, WINDOW), 0)
        lowest = first_key[r] + (ROWS - i * 128)
        allowed = (col >= lowest) & (col <= row + ROWS)
        bias[...] = jnp.where(allowed, 0.0, MASKED)
        kvw, vkw = kv[keys], vk[keys]

        def heads(q, k, v):
            s = nt(q[:, r].reshape(256, 128), k) * 0.125
            s = s + jnp.concatenate([bias[...], bias[...]], axis=0)
            e = jnp.exp(s - jnp.max(s, axis=-1, keepdims=True))
            total = jnp.sum(e, axis=-1, keepdims=True)
            return nn(e.astype(BF16), v) / total

        even = heads(q_even, kvw, vkw)
        odd = heads(q_odd, vkw, kvw)
        low = lax.broadcasted_iota(jnp.int32, (256, 128), 1) < 64
        both = jnp.where(low, even, odd).astype(BF16)
        att[y, r, pl.ds(0, 128)] = both[:128]
        att[y, r, pl.ds(128, 128)] = both[128:]

    def att_view(i):
        def view(member, first, rows):
            if member is None:
                return 128
            return att.at[member, pl.ds(i * 128 + first, rows)]

        return view

    def out_project(h):
        r = pl.ds(h * HALF, HALF)

        @pl.loop(0, NZ)
        def _(k):
            cols = pl.ds(pl.multiple_of(k * 256, 256), 256)
            total = jnp.zeros((HALF, 256), F32)
            for g in range(NY):
                w = w_out[g, k].reshape(256, 256)
                total = total + nt(att[g, r], w).astype(BF16).astype(F32)
            res[r, cols] = (tokens[r, cols].astype(F32) + total).astype(BF16)

    def expand(h, j):
        r = pl.ds(h * HALF, HALF)

        @pl.loop(0, 2)
        def _(n):
            cols = pl.ds(pl.multiple_of(n * 256, 256), 256)
            gate = nn(xn[r], w_gate[j, :, :, :, :, cols].reshape(WIDTH, 256))
            up = nn(xn[r], w_up[j, :, :, :, :, cols].reshape(WIDTH, 256))
            act = gate / (1.0 + jnp.exp(-gate)) * up
            hid[j, r, cols] = act.astype(BF16)

    def place(k):
        return net.zs((0, -1, 1, -2, 2, -3, 3, 4)[k])

    def contract(h, k):
        r = pl.ds(h * HALF, HALF)
        total = None
        for j in (0, 1):
            term = nt(hid[j, r], w_down[j, place(k)].reshape(COLS, SPAN))
            total = term if total is None else total + term
        part[h * UNITS + k] = total.astype(BF16)

    def reduce_y(h, k):
        u = h * UNITS + k
        ys, p = net.ys, part.at[u]
        b2 = BLOCK // 2
        cols = pl.ds(pl.multiple_of(place(k) * COLS, COLS), COLS)

        def rows(member, first, count):
            return pl.ds(pl.multiple_of(member * BLOCK + first, 16), count)

        a = net.send(p.at[rows(ys(2), 0, b2)], far_a.at[u], net.yp, FIRST)
        b = net.send(p.at[rows(ys(2), b2, b2)], far_b.at[u], net.ym, FIRST)
        yield
        arrived(a, b)
        ra, rb = rows(ys(1), 0, b2), rows(ys(-1), b2, b2)
        p[ra] = (p[ra].astype(F32) + far_a[u].astype(F32)).astype(BF16)
        a = net.send(p.at[rows(ys(1), 0, BLOCK)], near_p.at[u], net.yp, LATER)
        p[rb] = (p[rb].astype(F32) + far_b[u].astype(F32)).astype(BF16)
        b = net.send(p.at[rows(ys(-1), 0, BLOCK)], near_m.at[u], net.ym, LATER)
        yield
        arrived(a, b)
        own = rows(y, 0, BLOCK)
        total = p[own].astype(F32) + near_p[u].astype(F32) + near_m[u].astype(F32)

        def there(member, first, count):
            return out.at[pl.ds(pl.multiple_of(h * HALF + member * BLOCK + first, 16), count), cols]

        at = pl.ds(pl.multiple_of(h * HALF + y * BLOCK, 16), BLOCK)
        out[at, cols] = (res[at, cols].astype(F32) + total).astype(BF16)
        mine = there(y, 0, BLOCK)
        a, b = net.same(mine, net.yp, LATER), net.same(mine, net.ym, LATER)
        yield
        arrived(a, b)
        a = net.same(there(ys(-1), 0, b2), net.yp, LATER)
        b = net.same(there(ys(1), b2, b2), net.ym, LATER)
        yield
        arrived(a, b)
        yield

    routes = dict(
        q=w_q, k=w_kv, o=w_out.at[y], g0=w_gate.at[0], g1=w_gate.at[1],
        u0=w_up.at[0], u1=w_up.at[1], d0=w_down.at[0], d1=w_down.at[1],
    )
    moves = {
        n: (gather_direct if n in DIRECT else gather_zx if n in ROUND_Z_FIRST else gather_xz)(net, w)
        for n, w in routes.items()
    }
    moves["y"] = spread_out()
    moves.update({"s%d" % h: shift(h) for h in (0, 1)})
    moves.update({"a%d" % i: spread_y(net, att_view(i)) for i in range(6)})
    moves.update({"r%d%d" % (h, k): reduce_y(h, k) for h in (0, 1) for k in range(UNITS)})
    work = {
        "n": lambda i: norm_rows(tokens, attn_gain, i * 128, 128),
        "l": rope,
        "v": project_pair,
        "p": project_query,
        "t": attend,
        "w": out_project,
        "m": lambda h: norm_rows(res, mlp_gain, h * HALF, HALF),
        "e": expand,
        "c": contract,
    }
    for step in ORDER:
        if step in moves:
            net.step = step
            next(moves[step])
        else:
            work[step[0]](*(int(digit) for digit in step[1:]))
    assert net.slots <= SLOTS, net.slots
    for copy in net.copies[-SENDS:]:
        copy.wait_send()


def per_device(
    tokens, attn_gain, w_query, key_value_weight, w_out, mlp_gain, w_gate, w_up, w_down, doc_lengths
):
    shard = w_query.shape[0]
    args = (
        tokens, attn_gain.reshape(1, WIDTH), mlp_gain.reshape(1, WIDTH), doc_lengths.reshape(1, -1),
        jnp.asarray(rope_table()), w_query, key_value_weight.reshape(shard, 2, 64), jnp.swapaxes(w_out, 1, 2),
        w_gate, w_up, w_down.T,
    )
    vmem = pl.BlockSpec(memory_space=pltpu.VMEM)
    anywhere = pl.BlockSpec(memory_space=pl.ANY)
    big = (2, NZ, NX, 2, 32, SPAN)
    units = 2 * UNITS
    return pl.pallas_call(
        layer_kernel,
        out_shape=pltpu.VMEM((ROWS, WIDTH), BF16),
        in_specs=[anywhere, vmem, vmem, vmem, anywhere, vmem, vmem, vmem] + [anywhere] * 3,
        out_specs=vmem,
        scratch_shapes=[
            pltpu.VMEM((NZ, NX, 2, 32, 256), BF16),
            pltpu.VMEM((NZ, NX, 2, 32, 128), BF16),
            pltpu.VMEM((NY, NZ, NX, 2, 32, 256), BF16),
            pltpu.VMEM(big, BF16),
            pltpu.VMEM(big, BF16),
            pltpu.VMEM(big, BF16),
            pltpu.VMEM((ROWS, WIDTH), BF16),
            pltpu.VMEM((ROWS, WIDTH), BF16),
            pltpu.VMEM((2, ROWS, SPAN), BF16),
            pltpu.VMEM((2, ROWS, 128), BF16),
            pltpu.VMEM((2, ROWS, 128), BF16),
            pltpu.VMEM((2 * ROWS, 128), BF16),
            pltpu.VMEM((2 * ROWS, 128), BF16),
            pltpu.VMEM((128, WINDOW), F32),
            pltpu.VMEM((NY, ROWS, 256), BF16),
            pltpu.VMEM((units, HALF, COLS), BF16),
            pltpu.VMEM((units, BLOCK // 2, COLS), BF16),
            pltpu.VMEM((units, BLOCK // 2, COLS), BF16),
            pltpu.VMEM((units, BLOCK, COLS), BF16),
            pltpu.VMEM((units, BLOCK, COLS), BF16),
            pltpu.VMEM((ROWS, 128), F32),
            pltpu.VMEM((ROWS, 128), F32),
            pltpu.VMEM((ROWS, 1), jnp.int32),
            pltpu.VMEM((ROWS, WIDTH), BF16),
            pltpu.VMEM((ROWS, ROWS), BF16),
            pltpu.SemaphoreType.DMA((SENDS,)),
            pltpu.SemaphoreType.DMA((SLOTS,)),
            pltpu.SemaphoreType.DMA((8,)),
        ],
        compiler_params=pltpu.CompilerParams(
            collective_id=0, has_side_effects=True, vmem_limit_bytes=56 * 2**20
        ),
        name="layer",
    )(*args)


def solution(mesh):
    placed = (
        P("tok", None),
        P(),
        P("tok", "fsdp", None),
        P("tok", None, "fsdp", None),
        P("fsdp", None, "tok"),
        P(),
        P("tok", "fsdp"),
        P("tok", "fsdp"),
        P("fsdp", "tok"),
        P(),
    )
    return jax.shard_map(
        per_device, mesh=mesh, in_specs=placed, out_specs=P("tok", None), check_vma=False
    )
```

```python
import jax
import jax.numpy as jnp
import numpy as np
from jax import lax
from jax.experimental import pallas as pl
from jax.experimental.pallas import tpu as pltpu
from jax.sharding import PartitionSpec as P

ROPE_BASE = 500000.0
NORM_EPS = 1e-05
MASKED = -1e30
MESH = pl.DeviceIdType.MESH
F32, BF16 = jnp.float32, jnp.bfloat16

NZ, NX, NY = 8, 4, 4
ROWS = 768
WIDTH = 2048
HALF = 384
BLOCK = 96
SPAN = 512
COLS = 256
UNITS = 8
WINDOW = 896
SENDS, SLOTS = 64, 203
FIRST = ("k", "q")
LATER = ("o", "y", "g0", "g1", "u0", "u1")
SPREAD_DIRECT = True
DIRECT = ("k", "o",)
ROUND_Z_FIRST = ("q", "g0", "u1",)
ORDER = (
    "q", "o", "l", "g0", "n0", "n1", "n2", "n3", "q", "k", "o", "n4", "n5", "g0", "q", "k", "u0", "g1", "o",
    "u1", "q", "g0", "u0", "g1", "k", "u0", "o", "y", "u1", "q", "g1", "g0", "o", "k", "d1", "k", "v1",
    "s1", "d0", "u1", "u0", "q", "v0", "s0", "d1", "g1", "g0", "u1", "s1", "d0", "q", "u0", "d1", "s0", "q",
    "y", "p1", "g1", "u1", "p0", "t3", "a3", "u0", "g0", "d0", "t4", "a4", "t5", "a5", "d1", "y", "t0",
    "a0", "u1", "g1", "t1", "a1", "a3", "u0", "t2", "a2", "d0", "a4", "g0", "y", "u1", "u0", "d1", "a5",
    "w1", "a0", "d0", "u1", "g0", "g1", "m1", "e10", "a1", "d1", "g1", "e11", "a2", "d0", "c10", "r10",
    "c11", "r11", "c12", "r12", "c13", "r13", "d1", "c14", "r14", "w0", "r10", "r11", "r12", "r13", "r14",
    "d0", "d1", "c15", "r15", "c16", "r16", "m0", "e00", "r10", "r11", "r12", "r13", "d0", "c17", "r14",
    "r15", "r16", "r17", "e01", "r10", "r11", "c00", "r00", "r12", "c01", "r01", "c02", "r02", "r13", "c03",
    "r03", "c04", "r04", "r14", "c05", "r05", "r15", "c06", "r06", "c07", "r07", "r16", "r17", "r10", "r11",
    "r00", "r12", "r01", "r02", "r13", "r03", "r04", "r14", "r05", "r15", "r06", "r07", "r16", "r17", "r00",
    "r01", "r02", "r03", "r04", "r05", "r15", "r06", "r07", "r16", "r17", "r00", "r01", "r02", "r03", "r04",
    "r05", "r06", "r07", "r17", "r00", "r01", "r02", "r03", "r04", "r05", "r06", "r07",
)


def nt(a, b):
    return lax.dot_general(a, b, (((1,), (1,)), ((), ())), preferred_element_type=F32)


def nn(a, b):
    return jnp.dot(a, b, preferred_element_type=F32)


class Net:
    def __init__(self, send_sem, recv_sem):
        tok, self.y = lax.axis_index("tok"), lax.axis_index("fsdp")
        self.c = lax.rem(tok, 2)
        self.x = lax.rem(tok // 2, NX)
        self.z = tok // (2 * NX)
        self.send_sem, self.recv_sem = send_sem, recv_sem
        self.copies = []
        self.step, self.slots, self.used = None, 0, {}
        z, x, c, y = self.z, self.x, self.c, self.y

        def at(z, x, c):
            return (z * NX + x) * 2 + c

        self.zp = (at(self.zs(1), x, c), y)
        self.zm = (at(self.zs(-1), x, c), y)
        self.xp = (at(z, self.xs(1), c), y)
        self.xm = (at(z, self.xs(-1), c), y)
        self.sib = (at(z, x, 1 - c), y)
        self.z2p = (at(self.zs(2), x, c), y)
        self.z2m = (at(self.zs(-2), x, c), y)
        self.x2 = (at(z, self.xs(2), c), y)
        self.yp = (tok, self.ys(1))
        self.ym = (tok, self.ys(-1))
        self.y2 = (tok, self.ys(2))
        count = 2 * NX * NZ
        self.after = (lax.rem(tok + 1, count), y)
        self.before = (lax.rem(tok + count - 1, count), y)

    def zs(self, d):
        return lax.rem(self.z + NZ + d, NZ)

    def xs(self, d):
        return lax.rem(self.x + NX + d, NX)

    def ys(self, d):
        return lax.rem(self.y + NY + d, NY)

    def enter(self):
        self.partners = [
            self.zp, self.zm, self.xp, self.xm, self.sib, self.z2p, self.z2m, self.x2,
            self.yp, self.ym, self.y2, self.after, self.before,
        ]
        sem = pltpu.get_barrier_semaphore()
        for p in self.partners:
            pl.semaphore_signal(sem, 1, device_id=p, device_id_type=MESH)

    def entered(self):
        pl.semaphore_wait(pltpu.get_barrier_semaphore(), len(self.partners))

    def send(self, src, dst, to, again=()):
        i = len(self.copies)
        if i >= SENDS:
            self.copies[i - SENDS].wait_send()
        free = [n for n in again if self.used.get(n)]
        if free:
            slot = self.used[free[0]].pop()
        else:
            slot = self.slots
            self.slots += 1
            if not again:
                self.used.setdefault(self.step, []).append(slot)
        copy = pltpu.make_async_remote_copy(
            src_ref=src, dst_ref=dst, send_sem=self.send_sem.at[i % SENDS],
            recv_sem=self.recv_sem.at[slot], device_id=to, device_id_type=MESH,
        )
        copy.start()
        self.copies.append(copy)
        return copy

    def same(self, ref, to, again=()):
        return self.send(ref, ref, to, again)


def arrived(*copies):
    for copy in copies:
        copy.wait_recv()


def gather_xz(net, w):
    x, z, c, xs, zs = net.x, net.z, net.c, net.xs, net.zs
    a, b = net.same(w.at[z, x, c], net.xp), net.same(w.at[z, x, c], net.xm)
    yield
    arrived(a, b)
    a = net.same(w.at[z, xs(-1), c, pl.ds(0, 16)], net.xp)
    b = net.same(w.at[z, xs(1), c, pl.ds(16, 16)], net.xm)
    yield
    arrived(a, b)
    own = w.at[z, :, c]
    a, b, sib = net.same(own, net.zp), net.same(own, net.zm), [net.same(own, net.sib)]
    yield
    for hop in (1, 2):
        arrived(a, b, *sib)
        lo, hi = w.at[zs(-hop), :, c], w.at[zs(hop), :, c]
        a, b = net.same(lo, net.zp), net.same(hi, net.zm)
        sib = [net.same(lo, net.sib), net.same(hi, net.sib)]
        yield
    arrived(a, b, *sib)
    a = net.same(w.at[zs(-3), pl.ds(0, 2), c], net.zp)
    b = net.same(w.at[zs(3), pl.ds(2, 2), c], net.zm)
    sib = [net.same(w.at[zs(-3), :, c], net.sib), net.same(w.at[zs(3), :, c], net.sib)]
    yield
    arrived(a, b, *sib)
    last = net.same(w.at[zs(4), :, c], net.sib)
    yield
    arrived(last)
    yield


def gather_zx(net, w):
    x, z, c, xs, zs = net.x, net.z, net.c, net.xs, net.zs
    a, b = net.same(w.at[z, x, c], net.zp), net.same(w.at[z, x, c], net.zm)
    yield
    for hop in (1, 2):
        arrived(a, b)
        a, b = net.same(w.at[zs(-hop), x, c], net.zp), net.same(w.at[zs(hop), x, c], net.zm)
        yield
    arrived(a, b)
    a = net.same(w.at[zs(-3), x, c, pl.ds(0, 16)], net.zp)
    b = net.same(w.at[zs(3), x, c, pl.ds(16, 16)], net.zm)
    yield
    arrived(a, b)
    a, b = net.same(w.at[:, x, c], net.xp), net.same(w.at[:, x, c], net.xm)
    sib = [net.same(w.at[:, x, c], net.sib)]
    yield
    arrived(a, b)
    lo, hi = xs(-1), xs(1)
    a = net.same(w.at[pl.ds(0, 4), lo, c], net.xp)
    b = net.same(w.at[pl.ds(4, 4), hi, c], net.xm)
    sib += [net.same(w.at[:, lo, c], net.sib), net.same(w.at[:, hi, c], net.sib)]
    yield
    arrived(a, b)
    sib.append(net.same(w.at[:, xs(2), c], net.sib))
    yield
    arrived(*sib)
    yield


def gather_direct(net, w):
    x, z, c, xs, zs = net.x, net.z, net.c, net.xs, net.zs
    own = w.at[z, x, c]
    got = [net.same(own, p) for p in (net.xp, net.xm, net.x2)]
    yield
    arrived(*got)
    own = w.at[z, :, c]
    got = [net.same(own, p) for p in (net.zp, net.zm, net.z2p, net.z2m)]
    sib = [net.same(own, net.sib)]
    yield
    arrived(*got)
    lo, hi = w.at[zs(-2), :, c], w.at[zs(2), :, c]
    got = [
        net.same(lo, net.zp),
        net.same(hi, net.zm),
        net.same(w.at[zs(-2), pl.ds(0, 2), c], net.z2p),
        net.same(w.at[zs(2), pl.ds(2, 2), c], net.z2m),
    ]
    sib += [net.same(w.at[zs(d), :, c], net.sib) for d in (-2, -1, 1, 2)]
    yield
    arrived(*got)
    sib += [net.same(w.at[zs(d), :, c], net.sib) for d in (-3, 3, 4)]
    yield
    arrived(*sib)
    yield


def spread_y(net, view):
    rows = view(None, None, None)
    own = view(net.y, 0, rows)
    if SPREAD_DIRECT:
        got = [net.same(own, p) for p in (net.yp, net.ym, net.y2)]
        yield
        arrived(*got)
        yield
        return
    a, b = net.same(own, net.yp), net.same(own, net.ym)
    yield
    arrived(a, b)
    a = net.same(view(net.ys(-1), 0, rows // 2), net.yp)
    b = net.same(view(net.ys(1), rows // 2, rows // 2), net.ym)
    yield
    arrived(a, b)
    yield


def normed(x, gain):
    wide = x.astype(F32)
    factor = lax.rsqrt(jnp.mean(wide * wide, axis=-1, keepdims=True) + NORM_EPS)
    return (wide * factor * gain).astype(BF16)


def rope_table():
    f = np.float32(ROPE_BASE) ** (np.float32(-2.0) * np.arange(32, dtype=np.float32) / np.float32(64))
    angle = np.arange(ROWS, dtype=np.float32)[:, None] * f.astype(np.float32)[None, :]
    cos, sin = np.cos(angle.astype(np.float64)), np.sin(angle.astype(np.float64))
    left = np.concatenate([cos, cos, cos, cos, -sin, sin, -sin, sin], axis=1).astype(np.float32)
    terms = []
    for _ in range(3):
        terms.append(left.astype(BF16))
        left = left - terms[-1].astype(np.float32)
    return np.concatenate(terms, axis=1)


def layer_kernel(
    tokens_hbm, attn_gain, mlp_gain, lengths, table_hbm, s_query, s_pair, s_out, s_gate, s_up, s_down,
    out,
    w_q, w_kv, w_out, w_gate, w_up, w_down, xn, res, hid, q_even, q_odd, kv, vk, bias, att,
    part, far_a, far_b, near_p, near_m, cosine, sine, first_key, tokens, table, send_sem, recv_sem,
    own_sem,
):
    net = Net(send_sem, recv_sem)
    x, y, z, c = net.x, net.y, net.z, net.c
    net.enter()
    shards = [
        (s.at[:, pl.ds(j * SPAN, SPAN)], w.at[j, z, x, c])
        for w, s in ((w_gate, s_gate), (w_up, s_up), (w_down, s_down))
        for j in (0, 1)
    ]
    own = [
        pltpu.make_async_copy(src, dst, own_sem.at[i])
        for i, (src, dst) in enumerate([(tokens_hbm, tokens), (table_hbm, table)] + shards)
    ]
    for copy in own:
        copy.start()

    w_kv[z, x, c] = jnp.concatenate([s_pair[:, i, :] for i in range(2)], axis=1)
    w_q[z, x, c] = jnp.concatenate([s_query[:, h, :] for h in range(4)], axis=1)
    w_out[y, z, x, c] = jnp.concatenate([s_out[h] for h in range(4)], axis=1)
    for copy in own[2:]:
        copy.wait()
    net.entered()

    def spread_out():
        ys = net.ys

        def half(member, first):
            return w_out.at[member, pl.ds(first, 4), :, net.c]

        def whole(member):
            return w_out.at[member, :, :, net.c]

        a, b = net.same(whole(y), net.yp), net.same(whole(y), net.ym)
        yield
        arrived(a, b)
        a, b = net.same(half(ys(-1), 0), net.yp), net.same(half(ys(1), 4), net.ym)
        sib = [net.same(whole(ys(-1)), net.sib), net.same(whole(ys(1)), net.sib)]
        yield
        arrived(a, b)
        sib.append(net.same(whole(ys(2)), net.sib))
        yield
        arrived(*sib)
        yield

    def norm_rows(src, gain, first, count):
        if src is tokens and first == 0:
            own[0].wait()

        @pl.loop(0, count // 64)
        def _(i):
            r = pl.ds(pl.multiple_of(first + i * 64, 64), 64)
            xn[r] = normed(src[r], gain[...])

    def rope():
        own[1].wait()
        length = lengths[...].astype(F32)
        across = lax.broadcasted_iota(jnp.int32, (256, 256), 1)
        down = lax.broadcasted_iota(jnp.int32, (256, 256), 0)
        column = jnp.sum(jnp.where(across == down, length, 0.0), axis=1, keepdims=True)
        ends = jnp.sum(jnp.where(down <= across, column, 0.0), axis=0, keepdims=True)
        base = ((z * NX + x) * 2 + c) * ROWS
        local = lax.broadcasted_iota(jnp.int32, (ROWS, 1), 0)
        start = jnp.sum(
            jnp.where(ends <= (base + local).astype(F32), length, 0.0), axis=1, keepdims=True
        )
        begin = start.astype(jnp.int32) - base
        first_key[...] = begin
        onehot = (lax.broadcasted_iota(jnp.int32, (ROWS, ROWS), 1) == local - begin).astype(F32)
        turn = nn(onehot.astype(BF16), table[...])
        turn = turn[:, :256] + turn[:, 256:512] + turn[:, 512:]
        cosine[...] = turn[:, :128]
        sine[...] = turn[:, 128:]

    def turned(v, r):
        lead = lax.rem(lax.broadcasted_iota(jnp.int32, (HALF, 128), 1), 64) < 32
        swapped = jnp.where(lead, pltpu.roll(v, 96, 1), pltpu.roll(v, 32, 1))
        return v * cosine[r] + swapped * sine[r]

    def project_pair(h):
        r, there = pl.ds(h * HALF, HALF), pl.ds(ROWS + h * HALF, HALF)
        low = lax.broadcasted_iota(jnp.int32, (HALF, 128), 1) < 64
        prod = nn(xn[r], w_kv[...].reshape(WIDTH, 128))
        own = jnp.where(low, turned(prod, r), prod)
        kv[there] = own.astype(BF16)
        vk[there] = pltpu.roll(own, 64, 1).astype(BF16)

    def project_query(h):
        r = pl.ds(h * HALF, HALF)
        low = lax.broadcasted_iota(jnp.int32, (HALF, 128), 1) < 64
        prod = nn(xn[r], w_q[...].reshape(WIDTH, 256))
        for t in range(2):
            v = turned(prod[:, t * 128 : (t + 1) * 128], r)
            q_even[t, r] = jnp.where(low, v, 0.0).astype(BF16)
            q_odd[t, r] = jnp.where(low, 0.0, v).astype(BF16)

    def shift(h):
        there = pl.ds(h * HALF, HALF)
        copy = net.send(kv.at[pl.ds(ROWS + h * HALF, HALF)], kv.at[there], net.after)
        yield
        arrived(copy)
        vk[there] = pltpu.roll(kv[there].astype(F32), 64, 1).astype(BF16)
        yield

    def attend(i):
        r = pl.ds(i * 128, 128)
        keys = pl.ds(i * 128, WINDOW)
        col = lax.broadcasted_iota(jnp.int32, (128, WINDOW), 1)
        row = lax.broadcasted_iota(jnp.int32, (128, WINDOW), 0)
        lowest = first_key[r] + (ROWS - i * 128)
        allowed = (col >= lowest) & (col <= row + ROWS)
        bias[...] = jnp.where(allowed, 0.0, MASKED)
        kvw, vkw = kv[keys], vk[keys]

        def heads(q, k, v):
            s = nt(q[:, r].reshape(256, 128), k) * 0.125
            s = s + jnp.concatenate([bias[...], bias[...]], axis=0)
            e = jnp.exp(s - jnp.max(s, axis=-1, keepdims=True))
            total = jnp.sum(e, axis=-1, keepdims=True)
            return nn(e.astype(BF16), v) / total

        even = heads(q_even, kvw, vkw)
        odd = heads(q_odd, vkw, kvw)
        low = lax.broadcasted_iota(jnp.int32, (256, 128), 1) < 64
        both = jnp.where(low, even, odd).astype(BF16)
        att[y, r, pl.ds(0, 128)] = both[:128]
        att[y, r, pl.ds(128, 128)] = both[128:]

    def att_view(i):
        def view(member, first, rows):
            if member is None:
                return 128
            return att.at[member, pl.ds(i * 128 + first, rows)]

        return view

    def out_project(h):
        r = pl.ds(h * HALF, HALF)

        @pl.loop(0, NZ)
        def _(k):
            cols = pl.ds(pl.multiple_of(k * 256, 256), 256)
            total = jnp.zeros((HALF, 256), F32)
            for g in range(NY):
                w = w_out[g, k].reshape(256, 256)
                total = total + nt(att[g, r], w).astype(BF16).astype(F32)
            res[r, cols] = (tokens[r, cols].astype(F32) + total).astype(BF16)

    def expand(h, j):
        r = pl.ds(h * HALF, HALF)

        @pl.loop(0, 2)
        def _(n):
            cols = pl.ds(pl.multiple_of(n * 256, 256), 256)
            gate = nn(xn[r], w_gate[j, :, :, :, :, cols].reshape(WIDTH, 256))
            up = nn(xn[r], w_up[j, :, :, :, :, cols].reshape(WIDTH, 256))
            act = gate / (1.0 + jnp.exp(-gate)) * up
            hid[j, r, cols] = act.astype(BF16)

    def place(k):
        return net.zs((0, -1, 1, -2, 2, -3, 3, 4)[k])

    def contract(h, k):
        r = pl.ds(h * HALF, HALF)
        total = None
        for j in (0, 1):
            term = nt(hid[j, r], w_down[j, place(k)].reshape(COLS, SPAN))
            total = term if total is None else total + term
        part[h * UNITS + k] = total.astype(BF16)

    def reduce_y(h, k):
        u = h * UNITS + k
        ys, p = net.ys, part.at[u]
        b2 = BLOCK // 2
        cols = pl.ds(pl.multiple_of(place(k) * COLS, COLS), COLS)

        def rows(member, first, count):
            return pl.ds(pl.multiple_of(member * BLOCK + first, 16), count)

        a = net.send(p.at[rows(ys(2), 0, b2)], far_a.at[u], net.yp, FIRST)
        b = net.send(p.at[rows(ys(2), b2, b2)], far_b.at[u], net.ym, FIRST)
        yield
        arrived(a, b)
        ra, rb = rows(ys(1), 0, b2), rows(ys(-1), b2, b2)
        p[ra] = (p[ra].astype(F32) + far_a[u].astype(F32)).astype(BF16)
        a = net.send(p.at[rows(ys(1), 0, BLOCK)], near_p.at[u], net.yp, LATER)
        p[rb] = (p[rb].astype(F32) + far_b[u].astype(F32)).astype(BF16)
        b = net.send(p.at[rows(ys(-1), 0, BLOCK)], near_m.at[u], net.ym, LATER)
        yield
        arrived(a, b)
        own = rows(y, 0, BLOCK)
        total = p[own].astype(F32) + near_p[u].astype(F32) + near_m[u].astype(F32)

        def there(member, first, count):
            return out.at[pl.ds(pl.multiple_of(h * HALF + member * BLOCK + first, 16), count), cols]

        at = pl.ds(pl.multiple_of(h * HALF + y * BLOCK, 16), BLOCK)
        out[at, cols] = (res[at, cols].astype(F32) + total).astype(BF16)
        mine = there(y, 0, BLOCK)
        a, b = net.same(mine, net.yp, LATER), net.same(mine, net.ym, LATER)
        yield
        arrived(a, b)
        a = net.same(there(ys(-1), 0, b2), net.yp, LATER)
        b = net.same(there(ys(1), b2, b2), net.ym, LATER)
        yield
        arrived(a, b)
        yield

    routes = dict(
        q=w_q, k=w_kv, o=w_out.at[y], g0=w_gate.at[0], g1=w_gate.at[1],
        u0=w_up.at[0], u1=w_up.at[1], d0=w_down.at[0], d1=w_down.at[1],
    )
    moves = {
        n: (gather_direct if n in DIRECT else gather_zx if n in ROUND_Z_FIRST else gather_xz)(net, w)
        for n, w in routes.items()
    }
    moves["y"] = spread_out()
    moves.update({"s%d" % h: shift(h) for h in (0, 1)})
    moves.update({"a%d" % i: spread_y(net, att_view(i)) for i in range(6)})
    moves.update({"r%d%d" % (h, k): reduce_y(h, k) for h in (0, 1) for k in range(UNITS)})
    work = {
        "n": lambda i: norm_rows(tokens, attn_gain, i * 128, 128),
        "l": rope,
        "v": project_pair,
        "p": project_query,
        "t": attend,
        "w": out_project,
        "m": lambda h: norm_rows(res, mlp_gain, h * HALF, HALF),
        "e": expand,
        "c": contract,
    }
    for step in ORDER:
        if step in moves:
            net.step = step
            next(moves[step])
        else:
            work[step[0]](*(int(digit) for digit in step[1:]))
    assert net.slots <= SLOTS, net.slots
    for copy in net.copies[-SENDS:]:
        copy.wait_send()


def per_device(
    tokens, attn_gain, w_query, key_value_weight, w_out, mlp_gain, w_gate, w_up, w_down, doc_lengths
):
    shard = w_query.shape[0]
    args = (
        tokens, attn_gain.reshape(1, WIDTH), mlp_gain.reshape(1, WIDTH), doc_lengths.reshape(1, -1),
        jnp.asarray(rope_table()), w_query, key_value_weight.reshape(shard, 2, 64), jnp.swapaxes(w_out, 1, 2),
        w_gate, w_up, w_down.T,
    )
    vmem = pl.BlockSpec(memory_space=pltpu.VMEM)
    anywhere = pl.BlockSpec(memory_space=pl.ANY)
    big = (2, NZ, NX, 2, 32, SPAN)
    units = 2 * UNITS
    return pl.pallas_call(
        layer_kernel,
        out_shape=pltpu.VMEM((ROWS, WIDTH), BF16),
        in_specs=[anywhere, vmem, vmem, vmem, anywhere, vmem, vmem, vmem] + [anywhere] * 3,
        out_specs=vmem,
        scratch_shapes=[
            pltpu.VMEM((NZ, NX, 2, 32, 256), BF16),
            pltpu.VMEM((NZ, NX, 2, 32, 128), BF16),
            pltpu.VMEM((NY, NZ, NX, 2, 32, 256), BF16),
            pltpu.VMEM(big, BF16),
            pltpu.VMEM(big, BF16),
            pltpu.VMEM(big, BF16),
            pltpu.VMEM((ROWS, WIDTH), BF16),
            pltpu.VMEM((ROWS, WIDTH), BF16),
            pltpu.VMEM((2, ROWS, SPAN), BF16),
            pltpu.VMEM((2, ROWS, 128), BF16),
            pltpu.VMEM((2, ROWS, 128), BF16),
            pltpu.VMEM((2 * ROWS, 128), BF16),
            pltpu.VMEM((2 * ROWS, 128), BF16),
            pltpu.VMEM((128, WINDOW), F32),
            pltpu.VMEM((NY, ROWS, 256), BF16),
            pltpu.VMEM((units, HALF, COLS), BF16),
            pltpu.VMEM((units, BLOCK // 2, COLS), BF16),
            pltpu.VMEM((units, BLOCK // 2, COLS), BF16),
            pltpu.VMEM((units, BLOCK, COLS), BF16),
            pltpu.VMEM((units, BLOCK, COLS), BF16),
            pltpu.VMEM((ROWS, 128), F32),
            pltpu.VMEM((ROWS, 128), F32),
            pltpu.VMEM((ROWS, 1), jnp.int32),
            pltpu.VMEM((ROWS, WIDTH), BF16),
            pltpu.VMEM((ROWS, ROWS), BF16),
            pltpu.SemaphoreType.DMA((SENDS,)),
            pltpu.SemaphoreType.DMA((SLOTS,)),
            pltpu.SemaphoreType.DMA((8,)),
        ],
        compiler_params=pltpu.CompilerParams(
            collective_id=0, has_side_effects=True, vmem_limit_bytes=56 * 2**20
        ),
        name="layer",
    )(*args)


def solution(mesh):
    placed = (
        P("tok", None),
        P(),
        P("tok", "fsdp", None),
        P("tok", None, "fsdp", None),
        P("fsdp", None, "tok"),
        P(),
        P("tok", "fsdp"),
        P("tok", "fsdp"),
        P("fsdp", "tok"),
        P(),
    )
    return jax.shard_map(
        per_device, mesh=mesh, in_specs=placed, out_specs=P("tok", None), check_vma=False
    )
```

```python
import jax
import jax.numpy as jnp
import numpy as np
from jax import lax
from jax.experimental import pallas as pl
from jax.experimental.pallas import tpu as pltpu
from jax.sharding import PartitionSpec as P

ROPE_BASE = 500000.0
NORM_EPS = 1e-05
MASKED = -1e30
MESH = pl.DeviceIdType.MESH
F32, BF16 = jnp.float32, jnp.bfloat16

NZ, NX, NY = 8, 4, 4
ROWS = 768
WIDTH = 2048
HALF = 384
BLOCK = 96
SPAN = 512
COLS = 256
UNITS = 8
WINDOW = 896
SENDS, SLOTS = 64, 203
FIRST = ("k", "q")
LATER = ("o", "y", "g0", "g1", "u0", "u1")
SPREAD_DIRECT = True
DIRECT = ("k", "o",)
ROUND_Z_FIRST = ("q", "g0", "u1",)
ORDER = (
    "q", "o", "l", "g0", "n0", "n1", "n2", "n3", "q", "k", "o", "n4", "n5", "g0", "q", "k", "u0", "g1", "o",
    "u1", "q", "g0", "u0", "g1", "k", "u0", "o", "y", "u1", "q", "g1", "g0", "o", "k", "d1", "k", "v1",
    "s1", "d0", "u1", "u0", "q", "v0", "s0", "d1", "g1", "g0", "u1", "s1", "d0", "q", "u0", "d1", "s0", "q",
    "y", "p1", "g1", "u1", "p0", "t3", "a3", "u0", "g0", "d0", "t4", "a4", "t5", "a5", "d1", "y", "t0",
    "a0", "u1", "g1", "t1", "a1", "a3", "u0", "t2", "a2", "d0", "a4", "g0", "y", "u1", "u0", "d1", "a5",
    "w1", "a0", "d0", "u1", "g0", "g1", "m1", "e10", "a1", "d1", "g1", "e11", "a2", "d0", "c10", "r10",
    "c11", "r11", "c12", "r12", "c13", "r13", "d1", "c14", "r14", "w0", "r10", "r11", "r12", "r13", "r14",
    "d0", "d1", "c15", "r15", "c16", "r16", "m0", "e00", "r10", "r11", "r12", "r13", "d0", "c17", "r14",
    "r15", "r16", "r17", "e01", "r10", "r11", "c00", "r00", "r12", "c01", "r01", "c02", "r02", "r13", "c03",
    "r03", "c04", "r04", "r14", "c05", "r05", "r15", "c06", "r06", "c07", "r07", "r16", "r17", "r10", "r11",
    "r00", "r12", "r01", "r02", "r13", "r03", "r04", "r14", "r05", "r15", "r06", "r07", "r16", "r17", "r00",
    "r01", "r02", "r03", "r04", "r05", "r15", "r06", "r07", "r16", "r17", "r00", "r01", "r02", "r03", "r04",
    "r05", "r06", "r07", "r17", "r00", "r01", "r02", "r03", "r04", "r05", "r06", "r07",
)


def nt(a, b):
    return lax.dot_general(a, b, (((1,), (1,)), ((), ())), preferred_element_type=F32)


def nn(a, b):
    return jnp.dot(a, b, preferred_element_type=F32)


class Net:
    def __init__(self, send_sem, recv_sem):
        tok, self.y = lax.axis_index("tok"), lax.axis_index("fsdp")
        self.c = lax.rem(tok, 2)
        self.x = lax.rem(tok // 2, NX)
        self.z = tok // (2 * NX)
        self.send_sem, self.recv_sem = send_sem, recv_sem
        self.copies = []
        self.step, self.slots, self.used = None, 0, {}
        z, x, c, y = self.z, self.x, self.c, self.y

        def at(z, x, c):
            return (z * NX + x) * 2 + c

        self.zp = (at(self.zs(1), x, c), y)
        self.zm = (at(self.zs(-1), x, c), y)
        self.xp = (at(z, self.xs(1), c), y)
        self.xm = (at(z, self.xs(-1), c), y)
        self.sib = (at(z, x, 1 - c), y)
        self.z2p = (at(self.zs(2), x, c), y)
        self.z2m = (at(self.zs(-2), x, c), y)
        self.x2 = (at(z, self.xs(2), c), y)
        self.yp = (tok, self.ys(1))
        self.ym = (tok, self.ys(-1))
        self.y2 = (tok, self.ys(2))
        count = 2 * NX * NZ
        self.after = (lax.rem(tok + 1, count), y)
        self.before = (lax.rem(tok + count - 1, count), y)

    def zs(self, d):
        return lax.rem(self.z + NZ + d, NZ)

    def xs(self, d):
        return lax.rem(self.x + NX + d, NX)

    def ys(self, d):
        return lax.rem(self.y + NY + d, NY)

    def enter(self):
        self.partners = [
            self.zp, self.zm, self.xp, self.xm, self.sib, self.z2p, self.z2m, self.x2,
            self.yp, self.ym, self.y2, self.after, self.before,
        ]
        sem = pltpu.get_barrier_semaphore()
        for p in self.partners:
            pl.semaphore_signal(sem, 1, device_id=p, device_id_type=MESH)

    def entered(self):
        pl.semaphore_wait(pltpu.get_barrier_semaphore(), len(self.partners))

    def send(self, src, dst, to, again=()):
        i = len(self.copies)
        if i >= SENDS:
            self.copies[i - SENDS].wait_send()
        free = [n for n in again if self.used.get(n)]
        if free:
            slot = self.used[free[0]].pop()
        else:
            slot = self.slots
            self.slots += 1
            if not again:
                self.used.setdefault(self.step, []).append(slot)
        copy = pltpu.make_async_remote_copy(
            src_ref=src, dst_ref=dst, send_sem=self.send_sem.at[i % SENDS],
            recv_sem=self.recv_sem.at[slot], device_id=to, device_id_type=MESH,
        )
        copy.start()
        self.copies.append(copy)
        return copy

    def same(self, ref, to, again=()):
        return self.send(ref, ref, to, again)


def arrived(*copies):
    for copy in copies:
        copy.wait_recv()


def gather_xz(net, w):
    x, z, c, xs, zs = net.x, net.z, net.c, net.xs, net.zs
    a, b = net.same(w.at[z, x, c], net.xp), net.same(w.at[z, x, c], net.xm)
    yield
    arrived(a, b)
    a = net.same(w.at[z, xs(-1), c, pl.ds(0, 16)], net.xp)
    b = net.same(w.at[z, xs(1), c, pl.ds(16, 16)], net.xm)
    yield
    arrived(a, b)
    own = w.at[z, :, c]
    a, b, sib = net.same(own, net.zp), net.same(own, net.zm), [net.same(own, net.sib)]
    yield
    for hop in (1, 2):
        arrived(a, b, *sib)
        lo, hi = w.at[zs(-hop), :, c], w.at[zs(hop), :, c]
        a, b = net.same(lo, net.zp), net.same(hi, net.zm)
        sib = [net.same(lo, net.sib), net.same(hi, net.sib)]
        yield
    arrived(a, b, *sib)
    a = net.same(w.at[zs(-3), pl.ds(0, 2), c], net.zp)
    b = net.same(w.at[zs(3), pl.ds(2, 2), c], net.zm)
    sib = [net.same(w.at[zs(-3), :, c], net.sib), net.same(w.at[zs(3), :, c], net.sib)]
    yield
    arrived(a, b, *sib)
    last = net.same(w.at[zs(4), :, c], net.sib)
    yield
    arrived(last)
    yield


def gather_zx(net, w):
    x, z, c, xs, zs = net.x, net.z, net.c, net.xs, net.zs
    a, b = net.same(w.at[z, x, c], net.zp), net.same(w.at[z, x, c], net.zm)
    yield
    for hop in (1, 2):
        arrived(a, b)
        a, b = net.same(w.at[zs(-hop), x, c], net.zp), net.same(w.at[zs(hop), x, c], net.zm)
        yield
    arrived(a, b)
    a = net.same(w.at[zs(-3), x, c, pl.ds(0, 16)], net.zp)
    b = net.same(w.at[zs(3), x, c, pl.ds(16, 16)], net.zm)
    yield
    arrived(a, b)
    a, b = net.same(w.at[:, x, c], net.xp), net.same(w.at[:, x, c], net.xm)
    sib = [net.same(w.at[:, x, c], net.sib)]
    yield
    arrived(a, b)
    lo, hi = xs(-1), xs(1)
    a = net.same(w.at[pl.ds(0, 4), lo, c], net.xp)
    b = net.same(w.at[pl.ds(4, 4), hi, c], net.xm)
    sib += [net.same(w.at[:, lo, c], net.sib), net.same(w.at[:, hi, c], net.sib)]
    yield
    arrived(a, b)
    sib.append(net.same(w.at[:, xs(2), c], net.sib))
    yield
    arrived(*sib)
    yield


def gather_direct(net, w):
    x, z, c, xs, zs = net.x, net.z, net.c, net.xs, net.zs
    own = w.at[z, x, c]
    got = [net.same(own, p) for p in (net.xp, net.xm, net.x2)]
    yield
    arrived(*got)
    own = w.at[z, :, c]
    got = [net.same(own, p) for p in (net.zp, net.zm, net.z2p, net.z2m)]
    sib = [net.same(own, net.sib)]
    yield
    arrived(*got)
    lo, hi = w.at[zs(-2), :, c], w.at[zs(2), :, c]
    got = [
        net.same(lo, net.zp),
        net.same(hi, net.zm),
        net.same(w.at[zs(-2), pl.ds(0, 2), c], net.z2p),
        net.same(w.at[zs(2), pl.ds(2, 2), c], net.z2m),
    ]
    sib += [net.same(w.at[zs(d), :, c], net.sib) for d in (-2, -1, 1, 2)]
    yield
    arrived(*got)
    sib += [net.same(w.at[zs(d), :, c], net.sib) for d in (-3, 3, 4)]
    yield
    arrived(*sib)
    yield


def spread_y(net, view):
    rows = view(None, None, None)
    own = view(net.y, 0, rows)
    if SPREAD_DIRECT:
        got = [net.same(own, p) for p in (net.yp, net.ym, net.y2)]
        yield
        arrived(*got)
        yield
        return
    a, b = net.same(own, net.yp), net.same(own, net.ym)
    yield
    arrived(a, b)
    a = net.same(view(net.ys(-1), 0, rows // 2), net.yp)
    b = net.same(view(net.ys(1), rows // 2, rows // 2), net.ym)
    yield
    arrived(a, b)
    yield


def normed(x, gain):
    wide = x.astype(F32)
    factor = lax.rsqrt(jnp.mean(wide * wide, axis=-1, keepdims=True) + NORM_EPS)
    return (wide * factor * gain).astype(BF16)


def rope_table():
    f = np.float32(ROPE_BASE) ** (np.float32(-2.0) * np.arange(32, dtype=np.float32) / np.float32(64))
    angle = np.arange(ROWS, dtype=np.float32)[:, None] * f.astype(np.float32)[None, :]
    cos, sin = np.cos(angle.astype(np.float64)), np.sin(angle.astype(np.float64))
    left = np.concatenate([cos, cos, cos, cos, -sin, sin, -sin, sin], axis=1).astype(np.float32)
    terms = []
    for _ in range(3):
        terms.append(left.astype(BF16))
        left = left - terms[-1].astype(np.float32)
    return np.concatenate(terms, axis=1)


def layer_kernel(
    tokens_hbm, attn_gain, mlp_gain, lengths, table_hbm, s_query, s_pair, s_out, s_gate, s_up, s_down,
    out,
    w_q, w_kv, w_out, w_gate, w_up, w_down, xn, res, hid, q_even, q_odd, kv, vk, bias, att,
    part, far_a, far_b, near_p, near_m, cosine, sine, first_key, tokens, table, send_sem, recv_sem,
    own_sem,
):
    net = Net(send_sem, recv_sem)
    x, y, z, c = net.x, net.y, net.z, net.c
    net.enter()
    shards = [
        (s.at[:, pl.ds(j * SPAN, SPAN)], w.at[j, z, x, c])
        for w, s in ((w_gate, s_gate), (w_up, s_up), (w_down, s_down))
        for j in (0, 1)
    ]
    own = [
        pltpu.make_async_copy(src, dst, own_sem.at[i])
        for i, (src, dst) in enumerate([(tokens_hbm, tokens), (table_hbm, table)] + shards)
    ]
    for copy in own:
        copy.start()

    w_kv[z, x, c] = jnp.concatenate([s_pair[:, i, :] for i in range(2)], axis=1)
    w_q[z, x, c] = jnp.concatenate([s_query[:, h, :] for h in range(4)], axis=1)
    w_out[y, z, x, c] = jnp.concatenate([s_out[h] for h in range(4)], axis=1)
    for copy in own[2:]:
        copy.wait()
    net.entered()

    def spread_out():
        ys = net.ys

        def half(member, first):
            return w_out.at[member, pl.ds(first, 4), :, net.c]

        def whole(member):
            return w_out.at[member, :, :, net.c]

        a, b = net.same(whole(y), net.yp), net.same(whole(y), net.ym)
        yield
        arrived(a, b)
        a, b = net.same(half(ys(-1), 0), net.yp), net.same(half(ys(1), 4), net.ym)
        sib = [net.same(whole(ys(-1)), net.sib), net.same(whole(ys(1)), net.sib)]
        yield
        arrived(a, b)
        sib.append(net.same(whole(ys(2)), net.sib))
        yield
        arrived(*sib)
        yield

    def norm_rows(src, gain, first, count):
        if src is tokens and first == 0:
            own[0].wait()

        @pl.loop(0, count // 64)
        def _(i):
            r = pl.ds(pl.multiple_of(first + i * 64, 64), 64)
            xn[r] = normed(src[r], gain[...])

    def rope():
        own[1].wait()
        length = lengths[...].astype(F32)
        across = lax.broadcasted_iota(jnp.int32, (256, 256), 1)
        down = lax.broadcasted_iota(jnp.int32, (256, 256), 0)
        column = jnp.sum(jnp.where(across == down, length, 0.0), axis=1, keepdims=True)
        ends = jnp.sum(jnp.where(down <= across, column, 0.0), axis=0, keepdims=True)
        base = ((z * NX + x) * 2 + c) * ROWS
        local = lax.broadcasted_iota(jnp.int32, (ROWS, 1), 0)
        start = jnp.sum(
            jnp.where(ends <= (base + local).astype(F32), length, 0.0), axis=1, keepdims=True
        )
        begin = start.astype(jnp.int32) - base
        first_key[...] = begin
        onehot = (lax.broadcasted_iota(jnp.int32, (ROWS, ROWS), 1) == local - begin).astype(F32)
        turn = nn(onehot.astype(BF16), table[...])
        turn = turn[:, :256] + turn[:, 256:512] + turn[:, 512:]
        cosine[...] = turn[:, :128]
        sine[...] = turn[:, 128:]

    def turned(v, r):
        lead = lax.rem(lax.broadcasted_iota(jnp.int32, (HALF, 128), 1), 64) < 32
        swapped = jnp.where(lead, pltpu.roll(v, 96, 1), pltpu.roll(v, 32, 1))
        return v * cosine[r] + swapped * sine[r]

    def project_pair(h):
        r, there = pl.ds(h * HALF, HALF), pl.ds(ROWS + h * HALF, HALF)
        low = lax.broadcasted_iota(jnp.int32, (HALF, 128), 1) < 64
        prod = nn(xn[r], w_kv[...].reshape(WIDTH, 128))
        own = jnp.where(low, turned(prod, r), prod)
        kv[there] = own.astype(BF16)
        vk[there] = pltpu.roll(own, 64, 1).astype(BF16)

    def project_query(h):
        r = pl.ds(h * HALF, HALF)
        low = lax.broadcasted_iota(jnp.int32, (HALF, 128), 1) < 64
        prod = nn(xn[r], w_q[...].reshape(WIDTH, 256))
        for t in range(2):
            v = turned(prod[:, t * 128 : (t + 1) * 128], r)
            q_even[t, r] = jnp.where(low, v, 0.0).astype(BF16)
            q_odd[t, r] = jnp.where(low, 0.0, v).astype(BF16)

    def shift(h):
        there = pl.ds(h * HALF, HALF)
        copy = net.send(kv.at[pl.ds(ROWS + h * HALF, HALF)], kv.at[there], net.after)
        yield
        arrived(copy)
        vk[there] = pltpu.roll(kv[there].astype(F32), 64, 1).astype(BF16)
        yield

    def attend(i):
        r = pl.ds(i * 128, 128)
        keys = pl.ds(i * 128, WINDOW)
        col = lax.broadcasted_iota(jnp.int32, (128, WINDOW), 1)
        row = lax.broadcasted_iota(jnp.int32, (128, WINDOW), 0)
        lowest = first_key[r] + (ROWS - i * 128)
        allowed = (col >= lowest) & (col <= row + ROWS)
        bias[...] = jnp.where(allowed, 0.0, MASKED)
        kvw, vkw = kv[keys], vk[keys]

        def heads(q, k, v):
            s = nt(q[:, r].reshape(256, 128), k) * 0.125
            s = s + jnp.concatenate([bias[...], bias[...]], axis=0)
            e = jnp.exp(s - jnp.max(s, axis=-1, keepdims=True))
            total = jnp.sum(e, axis=-1, keepdims=True)
            return nn(e.astype(BF16), v) / total

        even = heads(q_even, kvw, vkw)
        odd = heads(q_odd, vkw, kvw)
        low = lax.broadcasted_iota(jnp.int32, (256, 128), 1) < 64
        both = jnp.where(low, even, odd).astype(BF16)
        att[y, r, pl.ds(0, 128)] = both[:128]
        att[y, r, pl.ds(128, 128)] = both[128:]

    def att_view(i):
        def view(member, first, rows):
            if member is None:
                return 128
            return att.at[member, pl.ds(i * 128 + first, rows)]

        return view

    def out_project(h):
        r = pl.ds(h * HALF, HALF)

        @pl.loop(0, NZ, unroll=2)
        def _(k):
            cols = pl.ds(pl.multiple_of(k * 256, 256), 256)
            total = jnp.zeros((HALF, 256), F32)
            for g in range(NY):
                w = w_out[g, k].reshape(256, 256)
                total = total + nt(att[g, r], w).astype(BF16).astype(F32)
            res[r, cols] = (tokens[r, cols].astype(F32) + total).astype(BF16)

    def expand(h, j):
        r = pl.ds(h * HALF, HALF)

        @pl.loop(0, 2, unroll=2)
        def _(n):
            cols = pl.ds(pl.multiple_of(n * 256, 256), 256)
            gate = nn(xn[r], w_gate[j, :, :, :, :, cols].reshape(WIDTH, 256))
            up = nn(xn[r], w_up[j, :, :, :, :, cols].reshape(WIDTH, 256))
            act = gate / (1.0 + jnp.exp(-gate)) * up
            hid[j, r, cols] = act.astype(BF16)

    def place(k):
        return net.zs((0, -1, 1, -2, 2, -3, 3, 4)[k])

    def contract(h, k):
        r = pl.ds(h * HALF, HALF)
        total = None
        for j in (0, 1):
            term = nt(hid[j, r], w_down[j, place(k)].reshape(COLS, SPAN))
            total = term if total is None else total + term
        part[h * UNITS + k] = total.astype(BF16)

    def reduce_y(h, k):
        u = h * UNITS + k
        ys, p = net.ys, part.at[u]
        b2 = BLOCK // 2
        cols = pl.ds(pl.multiple_of(place(k) * COLS, COLS), COLS)

        def rows(member, first, count):
            return pl.ds(pl.multiple_of(member * BLOCK + first, 16), count)

        a = net.send(p.at[rows(ys(2), 0, b2)], far_a.at[u], net.yp, FIRST)
        b = net.send(p.at[rows(ys(2), b2, b2)], far_b.at[u], net.ym, FIRST)
        yield
        arrived(a, b)
        ra, rb = rows(ys(1), 0, b2), rows(ys(-1), b2, b2)
        p[ra] = (p[ra].astype(F32) + far_a[u].astype(F32)).astype(BF16)
        a = net.send(p.at[rows(ys(1), 0, BLOCK)], near_p.at[u], net.yp, LATER)
        p[rb] = (p[rb].astype(F32) + far_b[u].astype(F32)).astype(BF16)
        b = net.send(p.at[rows(ys(-1), 0, BLOCK)], near_m.at[u], net.ym, LATER)
        yield
        arrived(a, b)
        own = rows(y, 0, BLOCK)
        total = p[own].astype(F32) + near_p[u].astype(F32) + near_m[u].astype(F32)

        def there(member, first, count):
            return out.at[pl.ds(pl.multiple_of(h * HALF + member * BLOCK + first, 16), count), cols]

        at = pl.ds(pl.multiple_of(h * HALF + y * BLOCK, 16), BLOCK)
        out[at, cols] = (res[at, cols].astype(F32) + total).astype(BF16)
        mine = there(y, 0, BLOCK)
        a, b = net.same(mine, net.yp, LATER), net.same(mine, net.ym, LATER)
        yield
        arrived(a, b)
        a = net.same(there(ys(-1), 0, b2), net.yp, LATER)
        b = net.same(there(ys(1), b2, b2), net.ym, LATER)
        yield
        arrived(a, b)
        yield

    routes = dict(
        q=w_q, k=w_kv, o=w_out.at[y], g0=w_gate.at[0], g1=w_gate.at[1],
        u0=w_up.at[0], u1=w_up.at[1], d0=w_down.at[0], d1=w_down.at[1],
    )
    moves = {
        n: (gather_direct if n in DIRECT else gather_zx if n in ROUND_Z_FIRST else gather_xz)(net, w)
        for n, w in routes.items()
    }
    moves["y"] = spread_out()
    moves.update({"s%d" % h: shift(h) for h in (0, 1)})
    moves.update({"a%d" % i: spread_y(net, att_view(i)) for i in range(6)})
    moves.update({"r%d%d" % (h, k): reduce_y(h, k) for h in (0, 1) for k in range(UNITS)})
    work = {
        "n": lambda i: norm_rows(tokens, attn_gain, i * 128, 128),
        "l": rope,
        "v": project_pair,
        "p": project_query,
        "t": attend,
        "w": out_project,
        "m": lambda h: norm_rows(res, mlp_gain, h * HALF, HALF),
        "e": expand,
        "c": contract,
    }
    for step in ORDER:
        if step in moves:
            net.step = step
            next(moves[step])
        else:
            work[step[0]](*(int(digit) for digit in step[1:]))
    assert net.slots <= SLOTS, net.slots
    for copy in net.copies[-SENDS:]:
        copy.wait_send()


def per_device(
    tokens, attn_gain, w_query, key_value_weight, w_out, mlp_gain, w_gate, w_up, w_down, doc_lengths
):
    shard = w_query.shape[0]
    args = (
        tokens, attn_gain.reshape(1, WIDTH), mlp_gain.reshape(1, WIDTH), doc_lengths.reshape(1, -1),
        jnp.asarray(rope_table()), w_query, key_value_weight.reshape(shard, 2, 64), jnp.swapaxes(w_out, 1, 2),
        w_gate, w_up, w_down.T,
    )
    vmem = pl.BlockSpec(memory_space=pltpu.VMEM)
    anywhere = pl.BlockSpec(memory_space=pl.ANY)
    big = (2, NZ, NX, 2, 32, SPAN)
    units = 2 * UNITS
    return pl.pallas_call(
        layer_kernel,
        out_shape=pltpu.VMEM((ROWS, WIDTH), BF16),
        in_specs=[anywhere, vmem, vmem, vmem, anywhere, vmem, vmem, vmem] + [anywhere] * 3,
        out_specs=vmem,
        scratch_shapes=[
            pltpu.VMEM((NZ, NX, 2, 32, 256), BF16),
            pltpu.VMEM((NZ, NX, 2, 32, 128), BF16),
            pltpu.VMEM((NY, NZ, NX, 2, 32, 256), BF16),
            pltpu.VMEM(big, BF16),
            pltpu.VMEM(big, BF16),
            pltpu.VMEM(big, BF16),
            pltpu.VMEM((ROWS, WIDTH), BF16),
            pltpu.VMEM((ROWS, WIDTH), BF16),
            pltpu.VMEM((2, ROWS, SPAN), BF16),
            pltpu.VMEM((2, ROWS, 128), BF16),
            pltpu.VMEM((2, ROWS, 128), BF16),
            pltpu.VMEM((2 * ROWS, 128), BF16),
            pltpu.VMEM((2 * ROWS, 128), BF16),
            pltpu.VMEM((128, WINDOW), F32),
            pltpu.VMEM((NY, ROWS, 256), BF16),
            pltpu.VMEM((units, HALF, COLS), BF16),
            pltpu.VMEM((units, BLOCK // 2, COLS), BF16),
            pltpu.VMEM((units, BLOCK // 2, COLS), BF16),
            pltpu.VMEM((units, BLOCK, COLS), BF16),
            pltpu.VMEM((units, BLOCK, COLS), BF16),
            pltpu.VMEM((ROWS, 128), F32),
            pltpu.VMEM((ROWS, 128), F32),
            pltpu.VMEM((ROWS, 1), jnp.int32),
            pltpu.VMEM((ROWS, WIDTH), BF16),
            pltpu.VMEM((ROWS, ROWS), BF16),
            pltpu.SemaphoreType.DMA((SENDS,)),
            pltpu.SemaphoreType.DMA((SLOTS,)),
            pltpu.SemaphoreType.DMA((8,)),
        ],
        compiler_params=pltpu.CompilerParams(
            collective_id=0, has_side_effects=True, vmem_limit_bytes=56 * 2**20
        ),
        name="layer",
    )(*args)


def solution(mesh):
    placed = (
        P("tok", None),
        P(),
        P("tok", "fsdp", None),
        P("tok", None, "fsdp", None),
        P("fsdp", None, "tok"),
        P(),
        P("tok", "fsdp"),
        P("tok", "fsdp"),
        P("fsdp", "tok"),
        P(),
    )
    return jax.shard_map(
        per_device, mesh=mesh, in_specs=placed, out_specs=P("tok", None), check_vma=False
    )
```
